128 devices in a mesh: seq: 16 (over y, x), tp: 8 (over z, core).
Axes of the slice: x: 4, y: 4, z: 4, core: 2. Of those that a mesh axis runs over, the one named last changes fastest.
Arguments:
- context: bfloat16 [128, 192, 1280], P('seq', 'tp'), may hold values from -6 to 6
- residual_in: bfloat16 [128, 192, 1280], P('seq', 'tp'), may hold values from -6 to 6
- out_weight: bfloat16 [1280, 1280], replicated, may hold values from -0.15625 to 0.15625
- final_norm_weight: float32 [1280], replicated, may hold values from 0.1 to 1.9
- final_norm_bias: float32 [1280], replicated, may hold values from -3 to 3
- adapter_in: bfloat16 [5120, 3584], P(None, 'tp'), may hold values from -0.078125 to 0.078125
- adapter_out: bfloat16 [3584, 3584], P('tp'), may hold values from -0.09375 to 0.09375
- emb_grad: bfloat16 [6144, 3584], P('seq', 'tp'), may hold values from -6 to 6
- group_offsets: int32 [128], replicated, may hold values from 0 to 6143, as said below
- group_frames: int32 [128], replicated, may hold values from 4 to 192, as said below
- group_owner: int32 [128], replicated, may hold values from 0 to 127, as said below
Outputs:
- d_context: bfloat16 [128, 192, 1280], P('seq', 'tp')
- d_residual: bfloat16 [128, 192, 1280], P('seq', 'tp')
- d_out_weight: float32 [1280, 1280], P(('seq', 'tp'))
- d_adapter_in: bfloat16 [5120, 3584], P('seq', 'tp')
- d_adapter_out: bfloat16 [3584, 3584], P('tp', 'seq')
The draws below stay inside these ranges and needn't reach their ends.
Inputs may be any that keep to these rules, and one draw needn't show every extreme that they name: `group_frames`: a multiple of 4; among groups 8 * q to 8 * q + 7 one has all 192 frames. `group_offsets`: the tokens of group k (group_frames[k] / 4 of them) lie within positions (k // 8) * 384 to (k // 8 + 1) * 384 - 1, in increasing order of k and without intersection. `group_owner`: each slot holds exactly one group; the 8 groups k // 8 = q lie in slots whose index // 8 are all different.
All inputs are finite; a program needn't handle non-finite values.
Results may differ from the reference program's by a relative error of at most 0.02.
Values may be sent and summed in bfloat16 or wider, within the bound.
No kernel may reach another device: no remote copies, remote signals or barrier semaphores. Data moves between devices by JAX's collectives and lax.ppermute only.
A program may use at most 128 MiB of HBM per device.

```python
import jax
import jax.numpy as jnp
from jax import lax

D = 3584
EW = 1280
SW = 5120
FR = 192
CT = 48
CPR = 8
TOK_DEV = 384
TOKENS = 6144
GROUPS = 128
N_SEQ = 16
N_TP = 8


def token_counts(key):
    counts = jax.random.randint(jax.random.fold_in(key, 11), (N_SEQ, CPR), 1, CT + 1)
    full_pick = jax.random.randint(jax.random.fold_in(key, 12), (N_SEQ,), 0, CPR)
    columns = jnp.arange(CPR, dtype=jnp.int32)
    return jnp.where(columns[None, :] == full_pick[:, None], CT, counts).astype(jnp.int32)


def draw_group_frames(key, part):
    counts = token_counts(key)
    return (4 * counts).reshape(-1).astype(jnp.int32)


def draw_group_offsets(key, part):
    counts = token_counts(key)
    key = jax.random.fold_in(key, 5)
    spare = TOK_DEV - jnp.sum(counts, axis=1)
    shares = jax.random.randint(key, (N_SEQ, CPR + 1), 1, 1000)
    gaps = spare[:, None] * shares // jnp.sum(shares, axis=1, keepdims=True)
    before = jnp.cumsum(gaps[:, :CPR], axis=1) + jnp.cumsum(counts, axis=1) - counts
    shard_base = jnp.arange(N_SEQ, dtype=jnp.int32)[:, None] * TOK_DEV
    return (shard_base + before).reshape(-1).astype(jnp.int32)


def draw_group_owner(key, part):
    key = jax.random.fold_in(key, 7)
    shuffled = jax.random.permutation(jax.random.fold_in(key, 1), N_SEQ).astype(jnp.int32)
    positions = jnp.arange(N_SEQ, dtype=jnp.int32)
    forced = (shuffled == N_SEQ - 1) | (shuffled == 1) | (shuffled == N_SEQ // 2)
    scores = jnp.where(forced, positions, N_SEQ + positions).astype(jnp.int32)
    order = jnp.argsort(scores, stable=True)
    row_shift = jnp.take(shuffled, order)[:CPR].astype(jnp.int32)
    column_shift = jax.random.randint(jax.random.fold_in(key, 2), (N_SEQ,), 0, CPR).astype(jnp.int32)
    shard_index = jnp.arange(N_SEQ, dtype=jnp.int32)[:, None]
    within = jnp.arange(CPR, dtype=jnp.int32)[None, :]
    source_row = (shard_index + row_shift[None, :]) % N_SEQ
    column = (within + jnp.take(column_shift, source_row)) % CPR
    return (source_row * CPR + column).reshape(-1).astype(jnp.int32)


def steps_of(key, shape, pieces, smallest, high):
    factor_of = 1.0
    for dim, blocks in pieces:
        steps = jax.random.uniform(jax.random.fold_in(jax.random.fold_in(key, 6), dim), (blocks,), jnp.float32, smallest / len(pieces), high / len(pieces))
        factor_of = factor_of * jnp.repeat(jnp.exp(steps), shape[dim] // blocks).reshape((-1,) + (1,) * (len(shape) - 1 - dim))
    return factor_of


def gaussian(own_key, extent, spread, limit, cuts=(), held_as=jnp.bfloat16):
    array = spread * jax.random.normal(own_key, extent, jnp.float32)
    if cuts:
        array = array * steps_of(own_key, extent, cuts, -0.22, 0.18)
    return jnp.clip(array, -limit, limit).astype(held_as)


def setup_inputs(seed: int = 0) -> dict:
    keys = jax.random.split(jax.random.key(seed), 12)
    context = gaussian(keys[0], (GROUPS, FR, EW), 1.0, 6.0, ((0, 16), (1, 8)))
    residual_in = gaussian(keys[1], (GROUPS, FR, EW), 1.0, 6.0, ((0, 16), (1, 8)))
    out_weight = gaussian(keys[2], (EW, EW), EW ** -0.5, 0.15625)
    final_norm_weight = jnp.clip(1.0 + 0.18 * jax.random.normal(keys[3], (EW,), jnp.float32), 0.1, 1.9)
    final_norm_bias = gaussian(keys[4], (EW,), 0.5, 3.0, (), jnp.float32)
    adapter_in = gaussian(keys[5], (SW, D), SW ** -0.5, 0.078125, ((1, 8),))
    adapter_out = gaussian(keys[6], (D, D), D ** -0.5, 0.09375, ((0, 8),))
    emb_grad = gaussian(keys[7], (TOKENS, D), 1.0, 6.0, ((0, 16), (1, 8)))
    group_offsets = draw_group_offsets(jax.random.fold_in(keys[11], 71), 0)
    group_frames = draw_group_frames(jax.random.fold_in(keys[11], 71), 0)
    group_owner = draw_group_owner(jax.random.fold_in(keys[11], 71), 0)
    return dict(context=context, residual_in=residual_in, out_weight=out_weight, final_norm_weight=final_norm_weight, final_norm_bias=final_norm_bias, adapter_in=adapter_in, adapter_out=adapter_out, emb_grad=emb_grad, group_offsets=group_offsets, group_frames=group_frames, group_owner=group_owner)


def gelu_exact(values):
    return 0.5 * values * (1.0 + jax.scipy.special.erf(values * 0.7071067811865476))

def gelu_slope(values):
    cumulative = 0.5 * (1.0 + jax.scipy.special.erf(values * 0.7071067811865476))
    density = jnp.exp(-0.5 * values * values) * 0.3989422804014327
    return cumulative + values * density

def reference(context, residual_in, out_weight, final_norm_weight, final_norm_bias, adapter_in, adapter_out, emb_grad, group_offsets, group_frames, group_owner):
    stream = residual_in.astype(jnp.float32) + jnp.einsum('sfe,eo->sfo', context.astype(jnp.float32), out_weight.astype(jnp.float32))
    centered_input = stream - lax.optimization_barrier(jnp.mean(stream, axis=-1, keepdims=True))
    inverse_deviation = lax.rsqrt(lax.optimization_barrier(jnp.mean(centered_input * centered_input, axis=-1, keepdims=True)) + 1e-05)
    normalized_input = centered_input * inverse_deviation
    encoder_output = (normalized_input * final_norm_weight + final_norm_bias).astype(jnp.bfloat16)
    stacked = encoder_output.reshape(GROUPS, CT, SW)[group_owner].reshape(GROUPS * CT, SW)
    token_steps = jnp.arange(CT, dtype=jnp.int32)
    places = jnp.clip(group_offsets[:, None] + token_steps[None, :], 0, TOKENS - 1).reshape(-1).astype(jnp.int32)
    live = (token_steps[None, :] < (group_frames // 4)[:, None]).reshape(-1)
    picked = jnp.take(emb_grad, places, axis=0)
    out_grad = jnp.where(live[:, None], picked, jnp.zeros_like(picked))
    preact = jnp.dot(stacked, adapter_in, preferred_element_type=jnp.float32)
    hidden = gelu_exact(preact).astype(jnp.bfloat16)
    hid_grad = jnp.dot(out_grad, adapter_out.T, preferred_element_type=jnp.float32)
    pre_grad = (hid_grad * gelu_slope(preact)).astype(jnp.bfloat16)
    block_rows = CPR * CT

    def accumulate(carry, block):
        first, second = carry
        rows_x, rows_p, rows_h, rows_g = block
        part_in = jnp.dot(rows_x.T, rows_p, preferred_element_type=jnp.float32).astype(jnp.bfloat16)
        part_out = jnp.dot(rows_h.T, rows_g, preferred_element_type=jnp.float32).astype(jnp.bfloat16)
        part_in, part_out = lax.optimization_barrier((part_in, part_out))
        return ((first + part_in.astype(jnp.float32), second + part_out.astype(jnp.float32)), None)
    blocks = (stacked.reshape(N_SEQ, block_rows, SW), pre_grad.reshape(N_SEQ, block_rows, D), hidden.reshape(N_SEQ, block_rows, D), out_grad.reshape(N_SEQ, block_rows, D))
    start = (jnp.zeros((SW, D), jnp.float32), jnp.zeros((D, D), jnp.float32))
    (grad_in, grad_out), _ = lax.scan(accumulate, start, blocks)
    part_width = D // N_TP
    row_grad = jnp.zeros((GROUPS * CT, SW), jnp.float32)
    for piece in range(N_TP):
        lower = piece * part_width
        term = jnp.dot(pre_grad[:, lower:lower + part_width], adapter_in[:, lower:lower + part_width].T, preferred_element_type=jnp.float32).astype(jnp.bfloat16)
        term = lax.optimization_barrier(term)
        row_grad = row_grad + term.astype(jnp.float32)
    row_grad = row_grad.astype(jnp.bfloat16).reshape(GROUPS, CT, SW)
    slot_grad = jnp.zeros((GROUPS, CT, SW), jnp.bfloat16).at[group_owner].set(row_grad)
    enc_grad = slot_grad.reshape(GROUPS, FR, EW).astype(jnp.float32)
    scaled_normed = enc_grad * final_norm_weight
    residual_gradient = inverse_deviation * (scaled_normed - lax.optimization_barrier(jnp.mean(scaled_normed, axis=-1, keepdims=True)) - normalized_input * lax.optimization_barrier(jnp.mean(scaled_normed * normalized_input, axis=-1, keepdims=True)))
    d_residual = residual_gradient.astype(jnp.bfloat16)
    d_context = jnp.einsum('sfo,eo->sfe', d_residual.astype(jnp.float32), out_weight.astype(jnp.float32)).astype(jnp.bfloat16)
    d_out_weight = jnp.einsum('sfe,sfo->eo', context.astype(jnp.float32), d_residual.astype(jnp.float32))
    return (d_context, d_residual, d_out_weight, grad_in.astype(jnp.bfloat16), grad_out.astype(jnp.bfloat16))
```

```python
import jax
import jax.numpy as jnp
from jax import lax
from jax.sharding import PartitionSpec as P

F32 = jnp.float32
BF16 = jnp.bfloat16
ZN, CN = 4, 2
YN, XN = 4, 4

CORE_SWAP = [(i, i ^ 1) for i in range(ZN * CN)]
Z_OUT = [(z * 2 + c, ((z + (1 if c == 0 else -1)) % ZN) * 2 + c) for z in range(ZN) for c in range(CN)]


def x_shift(step):
    return [(y * XN + x, y * XN + (x + step) % XN) for y in range(YN) for x in range(XN)]


def y_shift(step):
    return [(y * XN + x, ((y + step) % YN) * XN + x) for y in range(YN) for x in range(XN)]


def gelu_exact(values):
    return 0.5 * values * (1.0 + jax.scipy.special.erf(values * 0.7071067811865476))


def gelu_slope(values):
    cumulative = 0.5 * (1.0 + jax.scipy.special.erf(values * 0.7071067811865476))
    density = jnp.exp(-0.5 * values * values) * 0.3989422804014327
    return cumulative + values * density


def dotf(a, b, ca, cb):
    return lax.dot_general(a, b, (((ca,), (cb,)), ((), ())), preferred_element_type=F32)


def put(buf, block, index):
    return lax.dynamic_update_slice_in_dim(buf, block, index * block.shape[0], 0)


def tp_gather(block):
    rows = block.shape[0]
    t = lax.axis_index("tp")
    z, c = t // 2, t % 2
    buf = jnp.zeros((8 * rows, block.shape[1]), block.dtype)
    other = lax.ppermute(block, "tp", CORE_SWAP)
    pair = put(put(jnp.zeros((2 * rows, block.shape[1]), block.dtype), block, c), other, 1 - c)
    near = lax.ppermute(pair, "tp", Z_OUT)
    half = lax.dynamic_slice_in_dim(near, c * rows, rows, 0)
    far = lax.ppermute(half, "tp", Z_OUT)
    near_other = lax.ppermute(near, "tp", CORE_SWAP)
    far_other = lax.ppermute(far, "tp", CORE_SWAP)
    behind = (z + jnp.where(c == 0, 3, 1)) % 4
    ahead = (z + jnp.where(c == 0, 1, 3)) % 4
    across = (z + 2) % 4
    buf = put(buf, pair, z)
    buf = put(buf, near, behind)
    buf = put(buf, near_other, ahead)
    buf = put(buf, far, across * 2 + c)
    buf = put(buf, far_other, across * 2 + 1 - c)
    return buf


def add(a, b):
    return (a.astype(F32) + b.astype(F32)).astype(BF16)


def tp_scatter_sum(part):
    t = lax.axis_index("tp")
    z, c = t // 2, t % 2
    ahead = (z + jnp.where(c == 0, 1, 3)) % 4
    behind = (z + jnp.where(c == 0, 3, 1)) % 4
    across = (z + 2) % 4

    def take(index, count):
        return lax.dynamic_slice_in_dim(part, index, count, 0)

    give = jnp.concatenate([take(behind * 2, 2), take(across * 2 + 1 - c, 1), take(z * 2 + 1 - c, 1)])
    got = lax.ppermute(give, "tp", CORE_SWAP)
    pair = add(take(ahead * 2, 2), got[:2])
    far = add(take(across * 2 + c, 1), got[2:3])
    own = take(z * 2 + c, 1).astype(F32) + got[3:].astype(F32)
    far_in = lax.ppermute(far, "tp", Z_OUT)
    placed = jnp.where((jnp.arange(2) == c)[:, None, None], far_in.astype(F32), 0.0)
    pair = (pair.astype(F32) + placed).astype(BF16)
    near_in = lax.ppermute(pair, "tp", Z_OUT)
    mine = lax.dynamic_slice_in_dim(near_in, c, 1, 0)
    theirs = lax.dynamic_slice_in_dim(near_in, 1 - c, 1, 0)
    last = lax.ppermute(theirs, "tp", CORE_SWAP)
    return (own + mine.astype(F32) + last.astype(F32))[0]


def ring_scatter_sum(part, place, shift):
    def take(step):
        return lax.dynamic_index_in_dim(part, (place + step) % 4, 0, keepdims=False)

    half = part.shape[1] // 2
    far = take(2)
    up = lax.ppermute(far[:half], "seq", shift(1))
    down = lax.ppermute(far[half:], "seq", shift(-1))
    ahead, behind = take(1), take(3)
    ahead = jnp.concatenate([add(ahead[:half], up), ahead[half:]])
    behind = jnp.concatenate([behind[:half], add(behind[half:], down)])
    from_behind = lax.ppermute(ahead, "seq", shift(1))
    from_ahead = lax.ppermute(behind, "seq", shift(-1))
    return take(0).astype(F32) + from_behind.astype(F32) + from_ahead.astype(F32)


def seq_scatter_sum(part, x_first):
    s = lax.axis_index("seq")
    y, x = s // 4, s % 4
    rows, cols = part.shape[1:]
    grid = part.reshape(4, 4, rows, cols)
    if x_first:
        first = ring_scatter_sum(jnp.swapaxes(grid, 0, 1), x, x_shift)
        second = ring_scatter_sum(first.astype(BF16).reshape(4, 2, rows // 2, cols), y, y_shift)
    else:
        first = ring_scatter_sum(grid, y, y_shift)
        second = ring_scatter_sum(first.astype(BF16).reshape(4, 2, rows // 2, cols), x, x_shift)
    return second.reshape(rows, cols)


def per_device(
    context,
    residual_in,
    out_weight,
    final_norm_weight,
    final_norm_bias,
    adapter_in,
    adapter_out,
    emb_grad,
    group_offsets,
    group_frames,
    group_owner,
):
    s = lax.axis_index("seq")
    t = lax.axis_index("tp")
    context = context.reshape(192, 1280)
    residual_in = residual_in.reshape(192, 1280)

    my_groups = s * 8 + jnp.arange(8, dtype=jnp.int32)
    starts = jnp.take(group_offsets, my_groups) - s * 384
    counts = jnp.take(group_frames, my_groups) // 4
    goes = (jnp.take(group_owner, my_groups) // 8)[None, :] == jnp.arange(16, dtype=jnp.int32)[:, None]
    start_to = jnp.sum(jnp.where(goes, starts[None, :], 0), axis=1)
    count_to = jnp.sum(jnp.where(goes, counts[None, :], 0), axis=1)
    step = jnp.arange(48, dtype=jnp.int32)[None, :]
    place = jnp.where(step < count_to[:, None], start_to[:, None] + step, -1).reshape(768)
    pick = (place[:, None] == jnp.arange(384, dtype=jnp.int32)[None, :]).astype(BF16)
    parcels = dotf(pick, emb_grad, 1, 0).astype(BF16)
    arrived = lax.all_to_all(parcels, "seq", split_axis=0, concat_axis=0, tiled=True)

    stream = residual_in.astype(F32) + dotf(context, out_weight, 1, 0)
    centered = stream - jnp.mean(stream, axis=-1, keepdims=True)
    inverse_deviation = lax.rsqrt(jnp.mean(centered * centered, axis=-1, keepdims=True) + 1e-05)
    normalized = centered * inverse_deviation
    encoded = (normalized * final_norm_weight + final_norm_bias).astype(BF16).reshape(48, 5120)
    stacked = tp_gather(encoded)

    slot_ids = s * 8 + jnp.arange(8, dtype=jnp.int32)
    held = jnp.sum(
        jnp.where(group_owner[None, :] == slot_ids[:, None], jnp.arange(128, dtype=jnp.int32)[None, :], 0), axis=1
    )
    source = held // 8
    wanted = (
        source[None, :, None] * 48
        + jnp.arange(8, dtype=jnp.int32)[:, None, None] * 6
        + jnp.arange(6, dtype=jnp.int32)[None, None, :]
    ).reshape(384)
    route = (jnp.arange(768, dtype=jnp.int32)[:, None] == wanted[None, :]).astype(BF16)
    grad_here = dotf(arrived, route, 0, 0).astype(BF16)
    grad_t = tp_gather(grad_here)

    preact = dotf(adapter_in, stacked, 0, 1)
    hidden = gelu_exact(preact).astype(BF16)
    slope = gelu_slope(preact)
    hid_grad = dotf(adapter_out, grad_t, 1, 0)
    pre_grad = (hid_grad * slope).astype(BF16)

    row_part = dotf(pre_grad, adapter_in, 0, 1).astype(BF16)
    row_grad = tp_scatter_sum(row_part.reshape(8, 48, 5120))

    grad_in_part = dotf(stacked, pre_grad, 0, 1).astype(BF16)
    grad_out_part = dotf(grad_t, hidden, 1, 1).astype(BF16)
    grad_in = seq_scatter_sum(grad_in_part.reshape(16, 320, 448), True)
    grad_out = seq_scatter_sum(grad_out_part.reshape(16, 224, 448), False)

    enc_grad = row_grad.astype(BF16).astype(F32).reshape(192, 1280)
    scaled = enc_grad * final_norm_weight
    residual_gradient = inverse_deviation * (
        scaled
        - jnp.mean(scaled, axis=-1, keepdims=True)
        - normalized * jnp.mean(scaled * normalized, axis=-1, keepdims=True)
    )
    d_residual = residual_gradient.astype(BF16)
    d_context = dotf(d_residual, out_weight, 1, 1).astype(BF16)

    column = jnp.arange(1280, dtype=jnp.int32)
    target = (column // 160) * 10 + ((column % 160) // 10) * 80 + column % 10
    order = (jnp.arange(1280, dtype=jnp.int32)[:, None] == target[None, :]).astype(BF16)
    context_ordered = dotf(context, order, 1, 0).astype(BF16)
    weight_part = dotf(context_ordered, d_residual, 0, 0).astype(BF16)
    weight_tp = tp_scatter_sum(weight_part.reshape(8, 160, 1280)).astype(BF16)
    pieces = lax.all_to_all(weight_tp.reshape(16, 10, 1280), "seq", split_axis=0, concat_axis=0, tiled=True)
    d_out_weight = jnp.sum(pieces.astype(F32), axis=0)

    return (
        d_context.reshape(8, 24, 1280),
        d_residual.reshape(8, 24, 1280),
        d_out_weight,
        grad_in.astype(BF16),
        grad_out.T.astype(BF16),
    )


def solution(mesh):
    placed = (
        P("seq", "tp", None),
        P("seq", "tp", None),
        P(),
        P(),
        P(),
        P(None, "tp"),
        P("tp", None),
        P("seq", "tp"),
        P(),
        P(),
        P(),
    )
    return jax.shard_map(
        per_device,
        mesh=mesh,
        in_specs=placed,
        out_specs=(
            P("seq", "tp", None),
            P("seq", "tp", None),
            P(("seq", "tp"), None),
            P("seq", "tp"),
            P("tp", "seq"),
        ),
        check_vma=False,
    )
```

```python
import jax
import jax.numpy as jnp
from jax import lax
from jax.experimental import pallas as pl
from jax.experimental.pallas import tpu as pltpu
from jax.sharding import PartitionSpec as P

F32 = jnp.float32
BF16 = jnp.bfloat16
ZN, CN = 4, 2
YN, XN = 4, 4
TP = ZN * CN
PARAMS = pltpu.CompilerParams(vmem_limit_bytes=48 * 1024 * 1024)

CORE_SWAP = [(i, i ^ 1) for i in range(TP)]
Z_GROUPS = [[z * CN + c for z in range(ZN)] for c in range(CN)]


def z_shift(step):
    return [(z * CN + c, ((z + step) % ZN) * CN + c) for z in range(ZN) for c in range(CN)]


def x_shift(step):
    return [(y * XN + x, y * XN + (x + step) % XN) for y in range(YN) for x in range(XN)]


def y_shift(step):
    return [(y * XN + x, ((y + step) % YN) * XN + x) for y in range(YN) for x in range(XN)]


def gelu_parts(values):
    cumulative = 0.5 * (1.0 + lax.erf(values * 0.7071067811865476))
    density = jnp.exp(-0.5 * values * values) * 0.3989422804014327
    return values * cumulative, cumulative + values * density


def mm(a, b, ca=1, cb=0):
    return lax.dot_general(a, b, (((ca,), (cb,)), ((), ())), preferred_element_type=F32)


def iota(shape, dim):
    return lax.broadcasted_iota(jnp.int32, shape, dim)


def struct(shape, dtype):
    return jax.ShapeDtypeStruct(shape, dtype)


def whole(shape):
    return pl.BlockSpec(shape, lambda *_: (0,) * len(shape))


SMEM = pl.BlockSpec(memory_space=pltpu.SMEM)
VMEM = pl.BlockSpec(memory_space=pltpu.VMEM)


def cost(flops, nbytes, transcendentals=0):
    return pl.CostEstimate(flops=flops, bytes_accessed=nbytes, transcendentals=transcendentals)


def parcel_kernel(ids, offsets, frames, owner, grad, out):
    out[...] = jnp.zeros_like(out)
    s = ids[4]
    row, col = iota((48, 384), 0), iota((48, 384), 1)
    for k in range(8):
        group = s * 8 + k
        start = offsets[group] - s * 384
        count = lax.shift_right_logical(frames[group], 2)
        dest = lax.shift_right_logical(owner[group], 3)
        pick = jnp.where((row < count) & (col == row + start), 1.0, 0.0).astype(BF16)
        out[dest] = mm(pick, grad[...]).astype(BF16)


def parcels_of(ids, offsets, frames, owner, grad):
    return pl.pallas_call(
        parcel_kernel,
        out_shape=struct((16, 48, 448), BF16),
        in_specs=[SMEM, SMEM, SMEM, SMEM, VMEM],
        out_specs=VMEM,
        compiler_params=PARAMS,
        cost_estimate=cost(2 * 384 * 384 * 448, 2_000_000),
    )(ids, offsets, frames, owner, grad)


def select_kernel(ids, owner, arrived, keep, give):
    s, c = ids[4], ids[3]
    row = iota((192, 128), 0)
    z = lax.shift_right_logical(row * 1366, 16)
    rest = row - z * 48
    slot = lax.shift_right_logical(rest * 10923, 16)
    six = rest - slot * 6
    group = iota((192, 128), 1)
    source = jnp.sum(
        jnp.where(owner[...] == s * 8 + slot, lax.shift_right_logical(group, 3), 0), axis=1, keepdims=True
    )
    column = iota((192, 768), 1)
    tokens = arrived[...].reshape(768, 448)
    base = source * 48 + z[:, :1] * 12 + six[:, :1]
    for out, core in ((keep, c), (give, 1 - c)):
        route = jnp.where(column == base + core * 6, 1.0, 0.0).astype(BF16)
        out[...] = mm(route, tokens).astype(BF16)


def select_of(ids, owner, arrived):
    return pl.pallas_call(
        select_kernel,
        out_shape=(struct((192, 448), BF16), struct((192, 448), BF16)),
        in_specs=[SMEM, VMEM, VMEM],
        out_specs=(VMEM, VMEM),
        compiler_params=PARAMS,
        cost_estimate=cost(4 * 192 * 768 * 448, 1_500_000),
    )(ids, owner.reshape(1, 128), arrived)


def encode_kernel(context, residual, weight, gain, bias, stacked, normed, inverse, scratch):
    stream = residual[...].astype(F32) + mm(context[...], weight[...])
    centered = stream - jnp.mean(stream, axis=-1, keepdims=True)
    inv = lax.rsqrt(jnp.mean(centered * centered, axis=-1, keepdims=True) + 1e-05)
    norm = centered * inv
    normed[...] = norm
    inverse[...] = jnp.broadcast_to(inv, inverse.shape)
    encoded = norm * gain[...] + bias[...]
    for piece in range(10):
        scratch[piece] = encoded[:, piece * 128 : (piece + 1) * 128]
    for r in range(4):
        for piece in range(10):
            at = r * 1280 + piece * 128
            stacked[:, at : at + 128] = scratch[piece, pl.ds(r, 48, stride=4), :].astype(BF16)


def encode_of(context, residual, weight, gain, bias):
    return pl.pallas_call(
        encode_kernel,
        out_shape=(struct((48, 5120), BF16), struct((192, 1280), F32), struct((192, 128), F32)),
        in_specs=[VMEM] * 5,
        out_specs=(VMEM,) * 3,
        scratch_shapes=[pltpu.VMEM((10, 192, 128), F32)],
        compiler_params=PARAMS,
        cost_estimate=cost(2 * 192 * 1280 * 1280, 6_000_000),
    )(context, residual, weight, gain.reshape(1, 1280), bias.reshape(1, 1280))


def norm_back_kernel(rows, normed, inverse, gain, out, scratch):
    for r in range(4):
        for piece in range(10):
            at = r * 1280 + piece * 128
            total = rows[0, :, at : at + 128].astype(F32)
            for k in range(1, 4):
                total = total + rows[k, :, at : at + 128].astype(F32)
            scratch[piece, pl.ds(r, 48, stride=4), :] = total.astype(BF16).astype(F32)
    scaled = jnp.concatenate([scratch[piece] for piece in range(10)], axis=1) * gain[...]
    norm = normed[...]
    mean = jnp.mean(scaled, axis=-1, keepdims=True)
    along = jnp.mean(scaled * norm, axis=-1, keepdims=True)
    out[...] = (inverse[:, :1] * (scaled - mean - norm * along)).astype(BF16)


def norm_back_of(rows, normed, inverse, gain):
    return pl.pallas_call(
        norm_back_kernel,
        out_shape=struct((192, 1280), BF16),
        in_specs=[VMEM] * 4,
        out_specs=VMEM,
        scratch_shapes=[pltpu.VMEM((10, 192, 128), F32)],
        compiler_params=PARAMS,
        cost_estimate=cost(192 * 1280 * 20, 4_000_000),
    )(rows, normed, inverse, gain.reshape(1, 1280))


def preact_kernel(ids, b0, b1, b2, b3, own_w, other_w, stk, hid_own, hid_other, slope_own, slope_other, acc, acc_other):
    i = pl.program_id(0)
    for step, block in enumerate((b0, b1, b2, b3)):
        at = pl.multiple_of(lax.rem(ids[2] + step, 4) * 48, 16)
        stk[pl.ds(at, 48), :] = block[...]

    @pl.when(i == 0)
    def _():
        acc[...] = jnp.zeros_like(acc)
        acc_other[...] = jnp.zeros_like(acc_other)

    rows = stk[...]
    acc[...] += mm(rows, own_w[...])
    acc_other[...] += mm(rows, other_w[...])

    @pl.when(i == pl.num_programs(0) - 1)
    def _():
        hidden, slope = gelu_parts(acc[...])
        hid_own[...] = hidden.astype(BF16)
        slope_own[...] = slope
        hidden, slope = gelu_parts(acc_other[...])
        hid_other[...] = hidden.astype(BF16)
        slope_other[...] = slope


def preact_of(ids, blocks, own_w, other_w):
    return pl.pallas_call(
        preact_kernel,
        out_shape=(
            struct((192, 5120), BF16),
            struct((192, 448), BF16),
            struct((192, 448), BF16),
            struct((192, 448), F32),
            struct((192, 448), F32),
        ),
        grid=(5,),
        in_specs=[SMEM]
        + [pl.BlockSpec((48, 1024), lambda i: (0, i))] * 4
        + [pl.BlockSpec((1024, 448), lambda i: (i, 0))] * 2,
        out_specs=(pl.BlockSpec((192, 1024), lambda i: (0, i)),) + (whole((192, 448)),) * 4,
        scratch_shapes=[pltpu.VMEM((192, 448), F32)] * 2,
        compiler_params=PARAMS,
        cost_estimate=cost(4 * 192 * 5120 * 448, 13_000_000, 4 * 192 * 448),
    )(ids, *blocks, own_w, other_w)


def pre_grad_kernel(
    ids, g0, g1, g2, g3, out_own, out_other, in_own, in_other, hid_other, slope_own, slope_other,
    row_part, grads, pre_own, send, acc, acc_other,
):
    i = pl.program_id(0)

    @pl.when(i == 0)
    def _():
        acc[...] = jnp.zeros_like(acc)
        acc_other[...] = jnp.zeros_like(acc_other)

    for step, block in enumerate((g0, g1, g2, g3)):

        @pl.when(i == step)
        def _(block=block):
            piece = block[...]
            grads[...] = piece
            acc[...] += mm(piece, out_own[...], 1, 1)
            acc_other[...] += mm(piece, out_other[...], 1, 1)

    @pl.when(i == 3)
    def _():
        pre_own[...] = (acc[...] * slope_own[...]).astype(BF16)
        send[0:192, :] = (acc_other[...] * slope_other[...]).astype(BF16)
        send[192:384, :] = hid_other[...]

    @pl.when(i > 3)
    def _():
        row_part[...] = (mm(pre_own[...], in_own[...], 1, 1) + mm(send[0:192, :], in_other[...], 1, 1)).astype(BF16)


def pre_grad_of(ids, blocks, out_own, out_other, in_own, in_other, hid_other, slope_own, slope_other):
    def turn(i, ids):
        return (0, lax.rem(ids[2] + jnp.minimum(i, 3), 4))

    def later(i, ids):
        return (jnp.maximum(i - 4, 0), 0)

    return pl.pallas_call(
        pre_grad_kernel,
        out_shape=(
            struct((192, 5120), BF16),
            struct((192, 3584), BF16),
            struct((192, 448), BF16),
            struct((384, 448), BF16),
        ),
        grid_spec=pltpu.PrefetchScalarGridSpec(
            num_scalar_prefetch=1,
            grid=(9,),
            in_specs=[whole((192, 896))] * 4
            + [pl.BlockSpec((448, 896), turn)] * 2
            + [pl.BlockSpec((1024, 448), later)] * 2
            + [whole((192, 448))] * 3,
            out_specs=(
                pl.BlockSpec((192, 1024), lambda i, ids: (0, jnp.maximum(i - 4, 0))),
                pl.BlockSpec((192, 896), turn),
                whole((192, 448)),
                whole((384, 448)),
            ),
            scratch_shapes=[pltpu.VMEM((192, 448), F32)] * 2,
        ),
        compiler_params=PARAMS,
        cost_estimate=cost(4 * 192 * 448 * (3584 + 5120), 22_000_000),
    )(ids, *blocks, out_own, out_other, in_own, in_other, hid_other, slope_own, slope_other)


def weight_grad_kernel(ids, stk, stk_other, og, og_other, pre, hid, recv, *outs):
    i = pl.program_id(0)
    y_here, x_here = ids[0], ids[1]
    x_first, y_first = outs[:4], outs[4:]

    @pl.when(i < 8)
    def _():
        y = lax.shift_right_logical(i, 1)
        value = (mm(stk[...], pre[...], 0, 0) + mm(stk_other[...], recv[0:192, :], 0, 0)).astype(BF16)
        y_turn = lax.rem(y - y_here + 4, 4)
        for n in range(2):
            x = lax.rem(i, 2) * 2 + n
            x_turn = lax.rem(x - x_here + 4, 4)
            for k in range(4):

                @pl.when(x_turn == k)
                def _(k=k, n=n):
                    x_first[k][y] = value[n * 320 : n * 320 + 272]

                @pl.when(y_turn == k)
                def _(k=k, n=n, x=x):
                    y_first[k][x, 0:48, :] = value[n * 320 + 272 : n * 320 + 320]

    @pl.when(i >= 8)
    def _():
        y = i - 8
        value = (mm(og[...], hid[...], 0, 0) + mm(og_other[...], recv[192:384, :], 0, 0)).astype(BF16)
        y_turn = lax.rem(y - y_here + 4, 4)
        for k in range(4):

            @pl.when(y_turn == k)
            def _(k=k):
                for x in range(4):
                    y_first[k][x, 48:272, :] = value[x * 224 : x * 224 + 224]


def weight_grads_of(ids, stk, stk_other, og, og_other, pre, hid, recv):
    first = pl.BlockSpec((192, 640), lambda i, ids: (0, jnp.minimum(i, 7)))
    second = pl.BlockSpec((192, 896), lambda i, ids: (0, jnp.maximum(i - 8, 0)))
    return pl.pallas_call(
        weight_grad_kernel,
        out_shape=(struct((4, 272, 448), BF16),) * 8,
        grid_spec=pltpu.PrefetchScalarGridSpec(
            num_scalar_prefetch=1,
            grid=(12,),
            in_specs=[first, first, second, second, whole((192, 448)), whole((192, 448)), whole((384, 448))],
            out_specs=(whole((4, 272, 448)),) * 8,
        ),
        compiler_params=PARAMS,
        cost_estimate=cost(4 * 192 * 448 * (3584 + 5120), 16_000_000),
    )(ids, stk, stk_other, og, og_other, pre, hid, recv)


def spread_kernel(where, a, b, c, d, *outs):
    i = pl.program_id(0)
    value = (a[0].astype(F32) + b[0].astype(F32) + c[0].astype(F32) + d[0].astype(F32)).astype(BF16)
    for k in range(4):

        @pl.when(i == k)
        def _(k=k):
            outs[k][...] = value


def spread_of(where, parts):
    block = pl.BlockSpec((1, 272, 448), lambda i, where: (lax.rem(where[0] + i, 4), 0, 0))
    return pl.pallas_call(
        spread_kernel,
        out_shape=(struct((272, 448), BF16),) * 4,
        grid_spec=pltpu.PrefetchScalarGridSpec(
            num_scalar_prefetch=1,
            grid=(4,),
            in_specs=[block] * 4,
            out_specs=(whole((272, 448)),) * 4,
        ),
        compiler_params=PARAMS,
        cost_estimate=cost(16 * 272 * 448, 6_000_000),
    )(where, *parts)


def finish_kernel(a0, a1, a2, a3, b0, b1, b2, b3, grad_in, grad_out):
    first = a0[...].astype(F32) + a1[...].astype(F32) + a2[...].astype(F32) + a3[...].astype(F32)
    second = b0[...].astype(F32) + b1[...].astype(F32) + b2[...].astype(F32) + b3[...].astype(F32)
    grad_in[0:272, :] = first.astype(BF16)
    grad_in[272:320, :] = second[0:48].astype(BF16)
    grad_out[...] = second[48:272].T.astype(BF16)


def finish_of(first, second):
    return pl.pallas_call(
        finish_kernel,
        out_shape=(struct((320, 448), BF16), struct((448, 224), BF16)),
        in_specs=[VMEM] * 8,
        out_specs=(VMEM, VMEM),
        compiler_params=PARAMS,
        cost_estimate=cost(8 * 272 * 448, 3_000_000),
    )(*first, *second)


def ring_of(parts, shift):
    far = lax.ppermute(parts[2], "seq", shift(2))
    up = lax.ppermute(parts[1], "seq", shift(1))
    down = lax.ppermute(parts[3], "seq", shift(-1))
    return (parts[0], up, down, far)


def out_weight_kernel(ctx, ctx_other, grad, grad_other, out):
    out[...] = (mm(ctx[...], grad[...], 0, 0) + mm(ctx_other[...], grad_other[...], 0, 0)).astype(BF16)


def out_weight_of(ctx, ctx_other, grad, grad_other):
    block = pl.BlockSpec((192, 128), lambda i: (0, i))
    return pl.pallas_call(
        out_weight_kernel,
        out_shape=struct((640, 1280), BF16),
        grid=(5,),
        in_specs=[block, block, whole((192, 1280)), whole((192, 1280))],
        out_specs=pl.BlockSpec((128, 1280), lambda i: (i, 0)),
        compiler_params=PARAMS,
        cost_estimate=cost(4 * 192 * 640 * 1280, 4_000_000),
    )(ctx, ctx_other, grad, grad_other)


def swap(value):
    return lax.ppermute(value, "tp", CORE_SWAP)


def z_blocks(block):
    far = lax.ppermute(block, "tp", z_shift(2))
    behind = lax.ppermute(block, "tp", z_shift(1))
    ahead = lax.ppermute(block, "tp", z_shift(-1))
    return (block, ahead, far, behind)


def z_exchange(parts):
    return lax.all_to_all(parts, "tp", split_axis=0, concat_axis=0, axis_index_groups=Z_GROUPS, tiled=True)


def per_device(
    context,
    residual_in,
    out_weight,
    final_norm_weight,
    final_norm_bias,
    adapter_in,
    adapter_out,
    emb_grad,
    group_offsets,
    group_frames,
    group_owner,
):
    s = lax.axis_index("seq")
    t = lax.axis_index("tp")
    c = t % 2
    ids = jnp.stack([s // 4, s % 4, t // 2, c, s]).astype(jnp.int32)
    context = context.reshape(192, 1280)
    residual_in = residual_in.reshape(192, 1280)

    stacked_here, normed, inverse = encode_of(context, residual_in, out_weight, final_norm_weight, final_norm_bias)
    in_other = swap(adapter_in)
    out_other = swap(adapter_out)
    rows = z_blocks(stacked_here)

    parcels = parcels_of(ids, group_offsets, group_frames, group_owner, emb_grad)
    arrived = lax.all_to_all(parcels, "seq", split_axis=0, concat_axis=0, tiled=True)
    keep, give = select_of(ids, group_owner, arrived)
    got = swap(give)
    grad_pair = jnp.where(c == 0, jnp.concatenate([keep, got], axis=1), jnp.concatenate([got, keep], axis=1))
    grads = z_blocks(grad_pair)

    place = jnp.arange(1280, dtype=jnp.int32)
    core = (place // 640 + c) % 2
    target = (2 * ((place % 640) // 160) + core) * 10 + ((place % 160) // 10) * 80 + place % 10
    order = (jnp.arange(1280, dtype=jnp.int32)[:, None] == target[None, :]).astype(BF16)
    ordered = mm(context, order).astype(BF16)
    context_keep, context_got = ordered[:, :640], swap(ordered[:, 640:])

    stk, hid_own, hid_other, slope_own, slope_other = preact_of(ids, rows, adapter_in, in_other)
    stk_other = swap(stk)
    row_part, og, pre_own, send = pre_grad_of(
        ids, grads, adapter_out, out_other, adapter_in, in_other, hid_other, slope_own, slope_other
    )
    row_parts = z_exchange(row_part.reshape(4, 48, 5120))
    recv = swap(send)
    og_other = swap(og)

    parts = weight_grads_of(ids, stk, stk_other, og, og_other, pre_own, hid_own, recv)
    x_first = ring_of(parts[:4], x_shift)
    y_first = ring_of(parts[4:], y_shift)
    x_first = ring_of(spread_of(ids[0:1], x_first), y_shift)
    y_first = ring_of(spread_of(ids[1:2], y_first), x_shift)
    grad_in, grad_out = finish_of(x_first, y_first)

    d_residual = norm_back_of(row_parts, normed, inverse, final_norm_weight)
    residual_other = swap(d_residual)
    d_context = mm(d_residual, out_weight, 1, 1).astype(BF16)
    weight_part = out_weight_of(context_keep, context_got, d_residual, residual_other)
    weight_z = z_exchange(weight_part.reshape(4, 160, 1280))
    weight_z = jnp.sum(weight_z.astype(F32), axis=0).astype(BF16)
    pieces = lax.all_to_all(weight_z.reshape(16, 10, 1280), "seq", split_axis=0, concat_axis=0, tiled=True)
    d_out_weight = jnp.sum(pieces.astype(F32), axis=0)

    return (
        d_context.reshape(8, 24, 1280),
        d_residual.reshape(8, 24, 1280),
        d_out_weight,
        grad_in,
        grad_out,
    )


def solution(mesh):
    placed = (
        P("seq", "tp", None),
        P("seq", "tp", None),
        P(),
        P(),
        P(),
        P(None, "tp"),
        P("tp", None),
        P("seq", "tp"),
        P(),
        P(),
        P(),
    )
    return jax.shard_map(
        per_device,
        mesh=mesh,
        in_specs=placed,
        out_specs=(
            P("seq", "tp", None),
            P("seq", "tp", None),
            P(("seq", "tp"), None),
            P("seq", "tp"),
            P("tp", "seq"),
        ),
        check_vma=False,
    )
```

```python
import jax
import jax.numpy as jnp
from jax import lax
from jax.experimental import pallas as pl
from jax.experimental.pallas import tpu as pltpu
from jax.sharding import PartitionSpec as P

F32 = jnp.float32
BF16 = jnp.bfloat16
ZN, CN = 4, 2
YN, XN = 4, 4
TP = ZN * CN
PARAMS = pltpu.CompilerParams(vmem_limit_bytes=56 * 1024 * 1024)

CORE_SWAP = [(i, i ^ 1) for i in range(TP)]
Z_GROUPS = [[z * CN + c for z in range(ZN)] for c in range(CN)]


def z_shift(step):
    return [(z * CN + c, ((z + step) % ZN) * CN + c) for z in range(ZN) for c in range(CN)]


def x_shift(step):
    return [(y * XN + x, y * XN + (x + step) % XN) for y in range(YN) for x in range(XN)]


def y_shift(step):
    return [(y * XN + x, ((y + step) % YN) * XN + x) for y in range(YN) for x in range(XN)]


def gelu_parts(values):
    cumulative = 0.5 * (1.0 + lax.erf(values * 0.7071067811865476))
    density = jnp.exp(-0.5 * values * values) * 0.3989422804014327
    return values * cumulative, cumulative + values * density


def mm(a, b, ca=1, cb=0):
    return lax.dot_general(a, b, (((ca,), (cb,)), ((), ())), preferred_element_type=F32)


def iota(shape, dim):
    return lax.broadcasted_iota(jnp.int32, shape, dim)


def struct(shape, dtype):
    return jax.ShapeDtypeStruct(shape, dtype)


def whole(shape):
    return pl.BlockSpec(shape, lambda *_: (0,) * len(shape))


SMEM = pl.BlockSpec(memory_space=pltpu.SMEM)
VMEM = pl.BlockSpec(memory_space=pltpu.VMEM)


HINT = pl.CostEstimate(flops=1, bytes_accessed=1, transcendentals=0)
LONG = pl.CostEstimate(flops=40_000_000_000, bytes_accessed=100_000_000, transcendentals=1_000_000)


def parcel_kernel(ids, offsets, frames, owner, grad_t, out):
    out[...] = jnp.zeros_like(out)
    s = ids[4]
    row, col = iota((48, 384), 0), iota((48, 384), 1)
    picks, dests = [], []
    for k in range(8):
        group = s * 8 + k
        start = offsets[group] - s * 384
        count = lax.shift_right_logical(frames[group], 2)
        dests.append(lax.shift_right_logical(owner[group], 3))
        picks.append(jnp.where((row < count) & (col == row + start), 1.0, 0.0))
    tokens = mm(jnp.concatenate(picks).astype(BF16), grad_t[...], 1, 1).astype(BF16)
    for k in range(8):
        out[dests[k]] = tokens[k * 48 : k * 48 + 48]


def parcels_of(ids, offsets, frames, owner, grad_t):
    return pl.pallas_call(
        parcel_kernel,
        out_shape=struct((16, 48, 448), BF16),
        in_specs=[SMEM, SMEM, SMEM, SMEM, VMEM],
        out_specs=VMEM,
        compiler_params=PARAMS,
        cost_estimate=HINT,
    )(ids, offsets, frames, owner, grad_t)


def select_kernel(ids, owner, arrived, keep, give):
    s, c = ids[4], ids[3]
    row = iota((192, 128), 0)
    z = lax.shift_right_logical(row * 1366, 16)
    rest = row - z * 48
    slot = lax.shift_right_logical(rest * 10923, 16)
    six = rest - slot * 6
    group = iota((192, 128), 1)
    source = jnp.sum(
        jnp.where(owner[...] == s * 8 + slot, lax.shift_right_logical(group, 3), 0), axis=1, keepdims=True
    )
    column = iota((192, 768), 1)
    tokens = arrived[...].reshape(768, 448)
    base = source * 48 + z[:, :1] * 12 + six[:, :1]
    for out, core in ((keep, c), (give, 1 - c)):
        route = jnp.where(column == base + core * 6, 1.0, 0.0).astype(BF16)
        out[...] = mm(route, tokens).astype(BF16)


def select_of(ids, owner, arrived):
    return pl.pallas_call(
        select_kernel,
        out_shape=(struct((192, 448), BF16), struct((192, 448), BF16)),
        in_specs=[SMEM, VMEM, VMEM],
        out_specs=(VMEM, VMEM),
        compiler_params=PARAMS,
        cost_estimate=HINT,
    )(ids, owner.reshape(1, 128), arrived)


def pair_kernel(ids, keep, got, out):
    first = ids[3] == 0
    both = jnp.concatenate(
        [jnp.where(first, keep[...], got[...]), jnp.where(first, got[...], keep[...])], axis=1
    )
    for k in range(4):
        out[k] = both


def pair_of(ids, keep, got):
    return pl.pallas_call(
        pair_kernel,
        out_shape=struct((4, 192, 896), BF16),
        in_specs=[SMEM, VMEM, VMEM],
        out_specs=VMEM,
        compiler_params=PARAMS,
        cost_estimate=HINT,
    )(ids, keep, got)


def encode_kernel(context, residual, weight, gain, bias, stacked, normed, inverse, scratch):
    stream = residual[...].astype(F32) + mm(context[...], weight[...])
    centered = stream - jnp.mean(stream, axis=-1, keepdims=True)
    inv = lax.rsqrt(jnp.mean(centered * centered, axis=-1, keepdims=True) + 1e-05)
    norm = centered * inv
    normed[...] = norm
    inverse[...] = jnp.broadcast_to(inv, inverse.shape)
    encoded = norm * gain[...] + bias[...]
    for piece in range(10):
        scratch[piece] = encoded[:, piece * 128 : (piece + 1) * 128]
    for r in range(4):
        for piece in range(10):
            at = r * 1280 + piece * 128
            stacked[:, at : at + 128] = scratch[piece, pl.ds(r, 48, stride=4), :].astype(BF16)


def encode_of(context, residual, weight, gain, bias):
    return pl.pallas_call(
        encode_kernel,
        out_shape=(struct((48, 5120), BF16), struct((192, 1280), F32), struct((192, 128), F32)),
        in_specs=[VMEM] * 5,
        out_specs=(VMEM,) * 3,
        scratch_shapes=[pltpu.VMEM((10, 192, 128), F32)],
        compiler_params=PARAMS,
        cost_estimate=HINT,
    )(context, residual, weight, gain.reshape(1, 1280), bias.reshape(1, 1280))


def norm_back_kernel(rows, normed, inverse, gain, out, scratch):
    for r in range(4):
        for piece in range(10):
            at = r * 1280 + piece * 128
            total = rows[0, :, at : at + 128].astype(F32)
            for k in range(1, 4):
                total = total + rows[k, :, at : at + 128].astype(F32)
            scratch[piece, pl.ds(r, 48, stride=4), :] = total.astype(BF16).astype(F32)
    scaled = jnp.concatenate([scratch[piece] for piece in range(10)], axis=1) * gain[...]
    norm = normed[...]
    mean = jnp.mean(scaled, axis=-1, keepdims=True)
    along = jnp.mean(scaled * norm, axis=-1, keepdims=True)
    out[...] = (inverse[:, :1] * (scaled - mean - norm * along)).astype(BF16)


def norm_back_of(rows, normed, inverse, gain):
    return pl.pallas_call(
        norm_back_kernel,
        out_shape=struct((192, 1280), BF16),
        in_specs=[VMEM] * 4,
        out_specs=VMEM,
        scratch_shapes=[pltpu.VMEM((10, 192, 128), F32)],
        compiler_params=PARAMS,
        cost_estimate=LONG,
    )(rows, normed, inverse, gain.reshape(1, 1280))


def preact_kernel(ids, b0, b1, b2, b3, own_w, other_w, stk, hid_own, hid_other, slope_own, slope_other, acc, acc_other):
    i = pl.program_id(0)
    for step, block in enumerate((b0, b1, b2, b3)):
        at = pl.multiple_of(lax.rem(ids[2] + step, 4) * 48, 16)
        stk[pl.ds(at, 48), :] = block[...]

    @pl.when(i == 0)
    def _():
        acc[...] = jnp.zeros_like(acc)
        acc_other[...] = jnp.zeros_like(acc_other)

    rows = stk[...]
    acc[...] += mm(own_w[...], rows, 1, 1)
    acc_other[...] += mm(other_w[...], rows, 1, 1)

    @pl.when(i == pl.num_programs(0) - 1)
    def _():
        hidden, slope = gelu_parts(acc[...])
        hid_own[...] = hidden.astype(BF16)
        slope_own[...] = slope
        hidden, slope = gelu_parts(acc_other[...])
        hid_other[...] = hidden.astype(BF16)
        slope_other[...] = slope


def preact_of(ids, blocks, own_w, other_w):
    return pl.pallas_call(
        preact_kernel,
        out_shape=(
            struct((192, 5120), BF16),
            struct((448, 192), BF16),
            struct((448, 192), BF16),
            struct((448, 192), F32),
            struct((448, 192), F32),
        ),
        grid=(5,),
        in_specs=[SMEM]
        + [pl.BlockSpec((48, 1024), lambda i: (0, i))] * 4
        + [pl.BlockSpec((448, 1024), lambda i: (0, i))] * 2,
        out_specs=(pl.BlockSpec((192, 1024), lambda i: (0, i)),) + (whole((448, 192)),) * 4,
        scratch_shapes=[pltpu.VMEM((448, 192), F32)] * 2,
        compiler_params=PARAMS,
        cost_estimate=HINT,
    )(ids, *blocks, own_w, other_w)


def pre_grad_kernel(
    og, out_own, out_other, hid_other, slope_own, slope_other,
    pre_own, send, turned, turned_other, acc, acc_other,
):
    i = pl.program_id(0)

    @pl.when(i == 0)
    def _():
        acc[...] = jnp.zeros_like(acc)
        acc_other[...] = jnp.zeros_like(acc_other)

    piece = og[0]
    acc[...] += mm(out_own[...], piece, 1, 1)
    acc_other[...] += mm(out_other[...], piece, 1, 1)

    @pl.when(i == 3)
    def _():
        own = acc[...] * slope_own[...]
        other = acc_other[...] * slope_other[...]
        pre_own[...] = own.astype(BF16)
        send[0:448, :] = other.astype(BF16)
        send[448:896, :] = hid_other[...]
        turned[...] = own.T.astype(BF16)
        turned_other[...] = other.T.astype(BF16)


def pre_grad_of(og, out_own, out_other, hid_other, slope_own, slope_other):
    wide = pl.BlockSpec((448, 896), lambda i: (0, i))
    return pl.pallas_call(
        pre_grad_kernel,
        out_shape=(
            struct((448, 192), BF16),
            struct((896, 192), BF16),
            struct((192, 448), BF16),
            struct((192, 448), BF16),
        ),
        grid=(4,),
        in_specs=[pl.BlockSpec((1, 192, 896), lambda i: (i, 0, 0)), wide, wide] + [whole((448, 192))] * 3,
        out_specs=(whole((448, 192)), whole((896, 192)), whole((192, 448)), whole((192, 448))),
        scratch_shapes=[pltpu.VMEM((448, 192), F32)] * 2,
        compiler_params=PARAMS,
        cost_estimate=HINT,
    )(og, out_own, out_other, hid_other, slope_own, slope_other)


def row_kernel(pre, pre_other, in_own, in_other, out):
    out[...] = (mm(pre[...], in_own[...]) + mm(pre_other[...], in_other[...])).astype(BF16)


def rows_of(pre, pre_other, in_own, in_other):
    wide = pl.BlockSpec((448, 1280), lambda i: (0, i))
    return pl.pallas_call(
        row_kernel,
        out_shape=struct((192, 5120), BF16),
        grid=(4,),
        in_specs=[whole((192, 448))] * 2 + [wide] * 2,
        out_specs=pl.BlockSpec((192, 1280), lambda i: (0, i)),
        compiler_params=PARAMS,
        cost_estimate=HINT,
    )(pre, pre_other, in_own, in_other)


def x_columns(stk, og, x, out):
    for y in range(4):
        out[:, y * 320 : y * 320 + 320] = stk[:, (4 * y + x) * 320 : (4 * y + x + 1) * 320]
        out[:, 1280 + y * 224 : 1504 + y * 224] = og[y, :, x * 224 : x * 224 + 224]


def weight_grad_kernel(ids, stk, stk_other, og, og_other, pre, hid, recv, *outs):
    i = pl.program_id(0)
    x_first, y_first = outs[:5], outs[5:10]
    picked, picked_other = outs[10:]
    for x in range(4):

        @pl.when(i == x)
        def _(x=x):
            x_columns(stk, og, x, picked)
            x_columns(stk_other, og_other, x, picked_other)

    across = jnp.concatenate(
        [
            mm(pre[0:224], picked[:, 0:1280]) + mm(recv[0:224], picked_other[:, 0:1280]),
            mm(hid[0:224], picked[:, 1280:2176]) + mm(recv[448:672], picked_other[:, 1280:2176]),
        ],
        axis=1,
    ).astype(BF16)
    at = pl.ds(pl.multiple_of(i * 1280, 128), 1280)
    down = jnp.concatenate(
        [
            mm(pre[224:448], stk[:, at]) + mm(recv[224:448], stk_other[:, at]),
            mm(hid[224:448], og[i]) + mm(recv[672:896], og_other[i]),
        ],
        axis=1,
    ).astype(BF16)
    x_turn = lax.rem(i - ids[1] + 4, 4)
    y_turn = lax.rem(i - ids[0] + 4, 4)
    for turn, dests, value in ((x_turn, x_first, across), (y_turn, y_first, down)):
        for dest, k in ((0, 0), (1, 1), (2, 3)):

            @pl.when(turn == k)
            def _(dest=dests[dest], value=value):
                dest[...] = value

        @pl.when(turn == 2)
        def _(dests=dests, value=value):
            dests[3][...] = value[0:112]
            dests[4][...] = value[112:224]


def weight_grads_of(ids, stk, stk_other, og, og_other, pre, hid, recv):
    once = pl.Buffered(buffer_count=1)

    def single(shape):
        return pl.BlockSpec(shape, lambda *_: (0,) * len(shape), pipeline_mode=once)

    shapes = [(224, 2176)] * 3 + [(112, 2176)] * 2
    return pl.pallas_call(
        weight_grad_kernel,
        out_shape=tuple(struct(shape, BF16) for shape in shapes * 2),
        grid=(4,),
        in_specs=[SMEM]
        + [single((192, 5120))] * 2
        + [single((4, 192, 896))] * 2
        + [single((448, 192)), single((448, 192)), single((896, 192))],
        out_specs=tuple(single(shape) for shape in shapes * 2),
        scratch_shapes=[pltpu.VMEM((192, 2176), BF16)] * 2,
        compiler_params=PARAMS,
        cost_estimate=LONG,
    )(ids, stk, stk_other, og, og_other, pre, hid, recv)


def bump_kernel(x_up, x_down, y_up, y_down, a, b, c, d, *outs):
    for part, got, out in zip((x_up, x_down, y_up, y_down), (a, b, c, d), outs, strict=True):
        out[...] = (part[...].astype(F32) + got[...].astype(F32)).astype(BF16)


def bump_of(x_up, x_down, y_up, y_down, got):
    first = pl.BlockSpec((112, 2176), lambda i: (0, 0))
    second = pl.BlockSpec((112, 2176), lambda i: (1, 0))
    sides = [first, second, first, second]
    return pl.pallas_call(
        bump_kernel,
        out_shape=(struct((224, 2176), BF16),) * 4,
        grid=(1,),
        in_specs=sides + [first] * 4,
        out_specs=tuple(sides),
        input_output_aliases={0: 0, 1: 1, 2: 2, 3: 3},
        compiler_params=PARAMS,
        cost_estimate=HINT,
    )(x_up, x_down, y_up, y_down, *got)


def spread_kernel(where, a, b, c, *outs):
    value = (a[...].astype(F32) + b[...].astype(F32) + c[...].astype(F32)).astype(BF16)
    for n in range(4):
        piece = jnp.concatenate(
            [value[:, n * 320 : n * 320 + 320], value[:, 1280 + n * 224 : 1280 + n * 224 + 224]], axis=1
        )
        turn = lax.rem(n - where[0] + 4, 4)
        for k in range(4):

            @pl.when(turn == k)
            def _(k=k, piece=piece):
                outs[k][...] = piece


def spread_of(where, parts):
    return pl.pallas_call(
        spread_kernel,
        out_shape=(struct((224, 544), BF16),) * 4,
        in_specs=[SMEM] + [VMEM] * 3,
        out_specs=(VMEM,) * 4,
        compiler_params=PARAMS,
        cost_estimate=HINT,
    )(where, *parts)


def finish_kernel(a0, a1, a2, a3, b0, b1, b2, b3, grad_in, grad_out):
    first = a0[...].astype(F32) + a1[...].astype(F32) + a2[...].astype(F32) + a3[...].astype(F32)
    second = b0[...].astype(F32) + b1[...].astype(F32) + b2[...].astype(F32) + b3[...].astype(F32)
    both = jnp.concatenate([first, second], axis=0)
    grad_in[...] = both[:, 0:320].T.astype(BF16)
    grad_out[...] = both[:, 320:544].astype(BF16)


def finish_of(first, second):
    return pl.pallas_call(
        finish_kernel,
        out_shape=(struct((320, 448), BF16), struct((448, 224), BF16)),
        in_specs=[VMEM] * 8,
        out_specs=(VMEM, VMEM),
        compiler_params=PARAMS,
        cost_estimate=HINT,
    )(*first, *second)


def weight_sum_kernel(parts, out):
    total = parts[0].astype(F32)
    for k in range(1, 4):
        total = total + parts[k].astype(F32)
    out[...] = jnp.zeros_like(out)
    for n in range(16):
        out[n, 0:10, :] = total[n * 10 : n * 10 + 10].astype(BF16)


def weight_sum_of(parts):
    return pl.pallas_call(
        weight_sum_kernel,
        out_shape=struct((16, 16, 1280), BF16),
        in_specs=[VMEM],
        out_specs=VMEM,
        compiler_params=PARAMS,
        cost_estimate=HINT,
    )(parts)


def ring_of(parts, shift):
    far = lax.ppermute(parts[2], "seq", shift(2))
    up = lax.ppermute(parts[1], "seq", shift(1))
    down = lax.ppermute(parts[3], "seq", shift(-1))
    return (parts[0], up, down, far)


def order_kernel(target, context, out):
    pick = jnp.where(iota((1280, 256), 0) == target[...], 1.0, 0.0).astype(BF16)
    out[...] = mm(context[...], pick).astype(BF16)


def order_of(target, context):
    return pl.pallas_call(
        order_kernel,
        out_shape=struct((192, 1280), BF16),
        grid=(5,),
        in_specs=[pl.BlockSpec((1, 256), lambda i: (0, i)), whole((192, 1280))],
        out_specs=pl.BlockSpec((192, 256), lambda i: (0, i)),
        compiler_params=PARAMS,
        cost_estimate=LONG,
    )(target.reshape(1, 1280), context)


def out_weight_kernel(ctx, ctx_other, grad, grad_other, out):
    out[...] = (mm(ctx[...], grad[...], 0, 0) + mm(ctx_other[...], grad_other[...], 0, 0)).astype(BF16)


def out_weight_of(ctx, ctx_other, grad, grad_other):
    block = pl.BlockSpec((192, 128), lambda i: (0, i))
    return pl.pallas_call(
        out_weight_kernel,
        out_shape=struct((640, 1280), BF16),
        grid=(5,),
        in_specs=[block, block, whole((192, 1280)), whole((192, 1280))],
        out_specs=pl.BlockSpec((128, 1280), lambda i: (i, 0)),
        compiler_params=PARAMS,
        cost_estimate=HINT,
    )(ctx, ctx_other, grad, grad_other)


def swap(value):
    return lax.ppermute(value, "tp", CORE_SWAP)


def z_blocks(block):
    far = lax.ppermute(block, "tp", z_shift(2))
    behind = lax.ppermute(block, "tp", z_shift(1))
    ahead = lax.ppermute(block, "tp", z_shift(-1))
    return (block, ahead, far, behind)


def z_exchange(parts):
    return lax.all_to_all(parts, "tp", split_axis=0, concat_axis=0, axis_index_groups=Z_GROUPS, tiled=True)


def per_device(
    context,
    residual_in,
    out_weight,
    final_norm_weight,
    final_norm_bias,
    adapter_in,
    adapter_out,
    emb_grad,
    group_offsets,
    group_frames,
    group_owner,
):
    s = lax.axis_index("seq")
    t = lax.axis_index("tp")
    c = t % 2
    ids = jnp.stack([s // 4, s % 4, t // 2, c, s]).astype(jnp.int32)
    context = context.reshape(192, 1280)
    residual_in = residual_in.reshape(192, 1280)

    in_own = adapter_in.T
    in_other = swap(in_own)
    out_other = swap(adapter_out)

    parcels = parcels_of(ids, group_offsets, group_frames, group_owner, emb_grad.T)
    arrived = lax.all_to_all(parcels, "seq", split_axis=0, concat_axis=0, tiled=True)
    context, _ = lax.optimization_barrier((context, parcels))
    stacked_here, normed, inverse = encode_of(context, residual_in, out_weight, final_norm_weight, final_norm_bias)
    rows = z_blocks(stacked_here)
    arrived, in_other, out_other, _ = lax.optimization_barrier((arrived, in_other, out_other, stacked_here))

    keep, give = select_of(ids, group_owner, arrived)
    got = swap(give)
    grad_pair = pair_of(ids, keep, got)
    og = z_exchange(grad_pair)

    place = jnp.arange(1280, dtype=jnp.int32)
    core = (place // 640 + c) % 2
    target = (2 * ((place % 640) // 160) + core) * 10 + ((place % 160) // 10) * 80 + place % 10
    ordered = order_of(target, context)
    context_keep, context_got = ordered[:, :640], swap(ordered[:, 640:])

    rows, _ = lax.optimization_barrier((rows, grad_pair))
    stk, hid_own, hid_other, slope_own, slope_other = preact_of(ids, rows, in_own, in_other)
    stk_other = swap(stk)
    og, _ = lax.optimization_barrier((og, ordered))
    og_other = swap(og)
    pre_own, send, pre_rows, pre_rows_other = pre_grad_of(
        og, adapter_out, out_other, hid_other, slope_own, slope_other
    )
    recv = swap(send)
    row_part = rows_of(pre_rows, pre_rows_other, in_own, in_other)
    row_parts = z_exchange(row_part.reshape(4, 48, 5120))

    pre_own, _ = lax.optimization_barrier((pre_own, row_part))
    parts = weight_grads_of(ids, stk, stk_other, og, og_other, pre_own, hid_own, recv)
    x_here, x_up, x_down, x_far, x_far2 = parts[:5]
    y_here, y_up, y_down, y_far, y_far2 = parts[5:]
    got = (
        lax.ppermute(x_far, "seq", x_shift(1)),
        lax.ppermute(x_far2, "seq", x_shift(-1)),
        lax.ppermute(y_far, "seq", y_shift(1)),
        lax.ppermute(y_far2, "seq", y_shift(-1)),
    )
    row_parts, got = lax.optimization_barrier((row_parts, got))

    d_residual = norm_back_of(row_parts, normed, inverse, final_norm_weight)
    residual_other = swap(d_residual)
    weight_part = out_weight_of(context_keep, context_got, d_residual, residual_other)
    d_context = mm(d_residual, out_weight, 1, 1).astype(BF16)
    weight_parts, _ = lax.optimization_barrier((z_exchange(weight_part.reshape(4, 160, 1280)), d_context))
    weight_z = weight_sum_of(weight_parts)
    pieces = lax.all_to_all(weight_z, "seq", split_axis=0, concat_axis=0, tiled=True)
    d_out_weight = jnp.sum(pieces.astype(F32), axis=0)[:10]

    x_up, x_down, y_up, y_down = bump_of(x_up, x_down, y_up, y_down, got)
    x_sums = (x_here, lax.ppermute(x_up, "seq", x_shift(1)), lax.ppermute(x_down, "seq", x_shift(-1)))
    y_sums = (y_here, lax.ppermute(y_up, "seq", y_shift(1)), lax.ppermute(y_down, "seq", y_shift(-1)))
    first = ring_of(spread_of(ids[0:1], x_sums), y_shift)
    second = ring_of(spread_of(ids[1:2], y_sums), x_shift)
    grad_in, grad_out = finish_of(first, second)

    return (
        d_context.reshape(8, 24, 1280),
        d_residual.reshape(8, 24, 1280),
        d_out_weight,
        grad_in,
        grad_out,
    )


def solution(mesh):
    placed = (
        P("seq", "tp", None),
        P("seq", "tp", None),
        P(),
        P(),
        P(),
        P(None, "tp"),
        P("tp", None),
        P("seq", "tp"),
        P(),
        P(),
        P(),
    )
    return jax.shard_map(
        per_device,
        mesh=mesh,
        in_specs=placed,
        out_specs=(
            P("seq", "tp", None),
            P("seq", "tp", None),
            P(("seq", "tp"), None),
            P("seq", "tp"),
            P("tp", "seq"),
        ),
        check_vma=False,
    )
```

```python
import jax
import jax.numpy as jnp
from jax import lax
from jax.experimental import pallas as pl
from jax.experimental.pallas import tpu as pltpu
from jax.sharding import PartitionSpec as P

F32 = jnp.float32
BF16 = jnp.bfloat16
ZN, CN = 4, 2
YN, XN = 4, 4
TP = ZN * CN
PARAMS = pltpu.CompilerParams(vmem_limit_bytes=56 * 1024 * 1024)
SMALL = pltpu.CompilerParams(vmem_limit_bytes=20 * 1024 * 1024)

CORE_SWAP = [(i, i ^ 1) for i in range(TP)]
Z_GROUPS = [[z * CN + c for z in range(ZN)] for c in range(CN)]


def z_shift(step):
    return [(z * CN + c, ((z + step) % ZN) * CN + c) for z in range(ZN) for c in range(CN)]


def x_shift(step):
    return [(y * XN + x, y * XN + (x + step) % XN) for y in range(YN) for x in range(XN)]


def y_shift(step):
    return [(y * XN + x, ((y + step) % YN) * XN + x) for y in range(YN) for x in range(XN)]


def gelu_parts(values):
    cumulative = 0.5 * (1.0 + lax.erf(values * 0.7071067811865476))
    density = jnp.exp(-0.5 * values * values) * 0.3989422804014327
    return values * cumulative, cumulative + values * density


def mm(a, b, ca=1, cb=0):
    return lax.dot_general(a, b, (((ca,), (cb,)), ((), ())), preferred_element_type=F32)


def iota(shape, dim):
    return lax.broadcasted_iota(jnp.int32, shape, dim)


def struct(shape, dtype):
    return jax.ShapeDtypeStruct(shape, dtype)


def whole(shape):
    return pl.BlockSpec(shape, lambda *_: (0,) * len(shape))


SMEM = pl.BlockSpec(memory_space=pltpu.SMEM)
VMEM = pl.BlockSpec(memory_space=pltpu.VMEM)


HINT = pl.CostEstimate(flops=1, bytes_accessed=1, transcendentals=0)
LONG = pl.CostEstimate(flops=40_000_000_000, bytes_accessed=100_000_000, transcendentals=1_000_000)


def parcel_kernel(ids, offsets, frames, owner, grad_t, out):
    out[...] = jnp.zeros_like(out)
    s = ids[4]
    row, col = iota((48, 384), 0), iota((48, 384), 1)
    picks, dests = [], []
    for k in range(8):
        group = s * 8 + k
        start = offsets[group] - s * 384
        count = lax.shift_right_logical(frames[group], 2)
        dests.append(lax.shift_right_logical(owner[group], 3))
        picks.append(jnp.where((row < count) & (col == row + start), 1.0, 0.0))
    tokens = mm(jnp.concatenate(picks).astype(BF16), grad_t[...], 1, 1).astype(BF16)
    for k in range(8):
        out[dests[k]] = tokens[k * 48 : k * 48 + 48]


def parcels_of(ids, offsets, frames, owner, grad_t):
    return pl.pallas_call(
        parcel_kernel,
        out_shape=struct((16, 48, 448), BF16),
        in_specs=[SMEM, SMEM, SMEM, SMEM, VMEM],
        out_specs=VMEM,
        compiler_params=PARAMS,
        cost_estimate=HINT,
    )(ids, offsets, frames, owner, grad_t)


def select_kernel(ids, owner, arrived, keep, give):
    s, c = ids[4], ids[3]
    row = iota((192, 128), 0)
    z = lax.shift_right_logical(row * 1366, 16)
    rest = row - z * 48
    slot = lax.shift_right_logical(rest * 10923, 16)
    six = rest - slot * 6
    group = iota((192, 128), 1)
    source = jnp.sum(
        jnp.where(owner[...] == s * 8 + slot, lax.shift_right_logical(group, 3), 0), axis=1, keepdims=True
    )
    column = iota((192, 768), 1)
    tokens = arrived[...].reshape(768, 448)
    base = source * 48 + z[:, :1] * 12 + six[:, :1]
    for out, core in ((keep, c), (give, 1 - c)):
        route = jnp.where(column == base + core * 6, 1.0, 0.0).astype(BF16)
        out[...] = mm(route, tokens).astype(BF16)


def select_of(ids, owner, arrived):
    return pl.pallas_call(
        select_kernel,
        out_shape=(struct((192, 448), BF16), struct((192, 448), BF16)),
        in_specs=[SMEM, VMEM, VMEM],
        out_specs=(VMEM, VMEM),
        compiler_params=PARAMS,
        cost_estimate=HINT,
    )(ids, owner.reshape(1, 128), arrived)


def pair_kernel(ids, keep, got, out):
    first = ids[3] == 0
    both = jnp.concatenate(
        [jnp.where(first, keep[...], got[...]), jnp.where(first, got[...], keep[...])], axis=1
    )
    for k in range(4):
        out[k] = both


def pair_of(ids, keep, got):
    return pl.pallas_call(
        pair_kernel,
        out_shape=struct((4, 192, 896), BF16),
        in_specs=[SMEM, VMEM, VMEM],
        out_specs=VMEM,
        compiler_params=PARAMS,
        cost_estimate=HINT,
    )(ids, keep, got)


def encode_kernel(context, residual, weight, gain, bias, stacked, normed, inverse, scratch):
    stream = residual[...].astype(F32) + mm(context[...], weight[...])
    centered = stream - jnp.mean(stream, axis=-1, keepdims=True)
    inv = lax.rsqrt(jnp.mean(centered * centered, axis=-1, keepdims=True) + 1e-05)
    norm = centered * inv
    normed[...] = norm
    inverse[...] = jnp.broadcast_to(inv, inverse.shape)
    encoded = norm * gain[...] + bias[...]
    for piece in range(10):
        scratch[piece] = encoded[:, piece * 128 : (piece + 1) * 128]
    for r in range(4):
        for piece in range(10):
            at = r * 1280 + piece * 128
            stacked[:, at : at + 128] = scratch[piece, pl.ds(r, 48, stride=4), :].astype(BF16)


def encode_of(context, residual, weight, gain, bias):
    return pl.pallas_call(
        encode_kernel,
        out_shape=(struct((48, 5120), BF16), struct((192, 1280), F32), struct((192, 128), F32)),
        in_specs=[VMEM] * 5,
        out_specs=(VMEM,) * 3,
        scratch_shapes=[pltpu.VMEM((10, 192, 128), F32)],
        compiler_params=PARAMS,
        cost_estimate=HINT,
    )(context, residual, weight, gain.reshape(1, 1280), bias.reshape(1, 1280))


def norm_back_kernel(rows, normed, inverse, gain, out, scratch):
    for r in range(4):
        for piece in range(10):
            at = r * 1280 + piece * 128
            total = rows[0, :, at : at + 128].astype(F32)
            for k in range(1, 4):
                total = total + rows[k, :, at : at + 128].astype(F32)
            scratch[piece, pl.ds(r, 48, stride=4), :] = total.astype(BF16).astype(F32)
    scaled = jnp.concatenate([scratch[piece] for piece in range(10)], axis=1) * gain[...]
    norm = normed[...]
    mean = jnp.mean(scaled, axis=-1, keepdims=True)
    along = jnp.mean(scaled * norm, axis=-1, keepdims=True)
    out[...] = (inverse[:, :1] * (scaled - mean - norm * along)).astype(BF16)


def norm_back_of(rows, normed, inverse, gain):
    return pl.pallas_call(
        norm_back_kernel,
        out_shape=struct((192, 1280), BF16),
        in_specs=[VMEM] * 4,
        out_specs=VMEM,
        scratch_shapes=[pltpu.VMEM((10, 192, 128), F32)],
        compiler_params=SMALL,
        cost_estimate=LONG,
    )(rows, normed, inverse, gain.reshape(1, 1280))


def preact_kernel(ids, b0, b1, b2, b3, own_w, other_w, stk, hid_own, hid_other, slope_own, slope_other, acc, acc_other):
    i = pl.program_id(0)
    for step, block in enumerate((b0, b1, b2, b3)):
        at = pl.multiple_of(lax.rem(ids[2] + step, 4) * 48, 16)
        stk[pl.ds(at, 48), :] = block[...]

    @pl.when(i == 0)
    def _():
        acc[...] = jnp.zeros_like(acc)
        acc_other[...] = jnp.zeros_like(acc_other)

    rows = stk[...]
    acc[...] += mm(own_w[...], rows, 1, 1)
    acc_other[...] += mm(other_w[...], rows, 1, 1)

    @pl.when(i == pl.num_programs(0) - 1)
    def _():
        hidden, slope = gelu_parts(acc[...])
        hid_own[...] = hidden.astype(BF16)
        slope_own[...] = slope
        hidden, slope = gelu_parts(acc_other[...])
        hid_other[...] = hidden.astype(BF16)
        slope_other[...] = slope


def preact_of(ids, blocks, own_w, other_w):
    return pl.pallas_call(
        preact_kernel,
        out_shape=(
            struct((192, 5120), BF16),
            struct((448, 192), BF16),
            struct((448, 192), BF16),
            struct((448, 192), F32),
            struct((448, 192), F32),
        ),
        grid=(5,),
        in_specs=[SMEM]
        + [pl.BlockSpec((48, 1024), lambda i: (0, i))] * 4
        + [pl.BlockSpec((448, 1024), lambda i: (0, i))] * 2,
        out_specs=(pl.BlockSpec((192, 1024), lambda i: (0, i)),) + (whole((448, 192)),) * 4,
        scratch_shapes=[pltpu.VMEM((448, 192), F32)] * 2,
        compiler_params=PARAMS,
        cost_estimate=HINT,
    )(ids, *blocks, own_w, other_w)


def pre_grad_kernel(
    og, out_own, out_other, hid_other, slope_own, slope_other,
    pre_own, send, turned, turned_other, acc, acc_other,
):
    i = pl.program_id(0)

    @pl.when(i == 0)
    def _():
        acc[...] = jnp.zeros_like(acc)
        acc_other[...] = jnp.zeros_like(acc_other)

    piece = og[0]
    acc[...] += mm(out_own[...], piece, 1, 1)
    acc_other[...] += mm(out_other[...], piece, 1, 1)

    @pl.when(i == 3)
    def _():
        own = acc[...] * slope_own[...]
        other = acc_other[...] * slope_other[...]
        pre_own[...] = own.astype(BF16)
        send[0:448, :] = other.astype(BF16)
        send[448:896, :] = hid_other[...]
        turned[...] = own.T.astype(BF16)
        turned_other[...] = other.T.astype(BF16)


def pre_grad_of(og, out_own, out_other, hid_other, slope_own, slope_other):
    wide = pl.BlockSpec((448, 896), lambda i: (0, i))
    return pl.pallas_call(
        pre_grad_kernel,
        out_shape=(
            struct((448, 192), BF16),
            struct((896, 192), BF16),
            struct((192, 448), BF16),
            struct((192, 448), BF16),
        ),
        grid=(4,),
        in_specs=[pl.BlockSpec((1, 192, 896), lambda i: (i, 0, 0)), wide, wide] + [whole((448, 192))] * 3,
        out_specs=(whole((448, 192)), whole((896, 192)), whole((192, 448)), whole((192, 448))),
        scratch_shapes=[pltpu.VMEM((448, 192), F32)] * 2,
        compiler_params=PARAMS,
        cost_estimate=HINT,
    )(og, out_own, out_other, hid_other, slope_own, slope_other)


def row_kernel(pre, pre_other, in_own, in_other, out):
    out[...] = (mm(pre[...], in_own[...]) + mm(pre_other[...], in_other[...])).astype(BF16)


def rows_of(pre, pre_other, in_own, in_other):
    wide = pl.BlockSpec((448, 1280), lambda i: (0, i))
    return pl.pallas_call(
        row_kernel,
        out_shape=struct((192, 5120), BF16),
        grid=(4,),
        in_specs=[whole((192, 448))] * 2 + [wide] * 2,
        out_specs=pl.BlockSpec((192, 1280), lambda i: (0, i)),
        compiler_params=PARAMS,
        cost_estimate=HINT,
    )(pre, pre_other, in_own, in_other)


def x_columns(stk, og, x, out):
    for y in range(4):
        out[:, y * 320 : y * 320 + 320] = stk[:, (4 * y + x) * 320 : (4 * y + x + 1) * 320]
        out[:, 1280 + y * 224 : 1504 + y * 224] = og[y, :, x * 224 : x * 224 + 224]


def weight_grad_kernel(far, ids, stk, stk_other, og, og_other, pre, hid, recv, *outs):
    i = pl.program_id(0)
    turn = 2 if far else jnp.where(i == 2, 3, i)
    x_at, y_at = lax.rem(ids[1] + turn, 4), lax.rem(ids[0] + turn, 4)
    picked, picked_other = outs[-2:]
    for x in range(4):

        @pl.when(x_at == x)
        def _(x=x):
            x_columns(stk, og, x, picked)
            x_columns(stk_other, og_other, x, picked_other)

    across = jnp.concatenate(
        [
            mm(pre[0:224], picked[:, 0:1280]) + mm(recv[0:224], picked_other[:, 0:1280]),
            mm(hid[0:224], picked[:, 1280:2176]) + mm(recv[448:672], picked_other[:, 1280:2176]),
        ],
        axis=1,
    ).astype(BF16)
    at = pl.ds(pl.multiple_of(y_at * 1280, 128), 1280)
    down = jnp.concatenate(
        [
            mm(pre[224:448], stk[:, at]) + mm(recv[224:448], stk_other[:, at]),
            mm(hid[224:448], og[y_at]) + mm(recv[672:896], og_other[y_at]),
        ],
        axis=1,
    ).astype(BF16)
    if far:
        outs[0][...] = across[0:112]
        outs[1][...] = across[112:224]
        outs[2][...] = down[0:112]
        outs[3][...] = down[112:224]
        return
    for k in range(3):

        @pl.when(i == k)
        def _(k=k):
            outs[k][...] = across
            outs[3 + k][...] = down


def weight_grads_of(far, ids, stk, stk_other, og, og_other, pre, hid, recv):
    once = pl.Buffered(buffer_count=1)

    def single(shape):
        return pl.BlockSpec(shape, lambda *_: (0,) * len(shape), pipeline_mode=once)

    def kernel(*refs):
        weight_grad_kernel(far, *refs)

    shapes = [(112, 2176)] * 4 if far else [(224, 2176)] * 6
    return pl.pallas_call(
        kernel,
        out_shape=tuple(struct(shape, BF16) for shape in shapes),
        grid=(1 if far else 3,),
        in_specs=[SMEM]
        + [single((192, 5120))] * 2
        + [single((4, 192, 896))] * 2
        + [single((448, 192)), single((448, 192)), single((896, 192))],
        out_specs=tuple(single(shape) for shape in shapes),
        scratch_shapes=[pltpu.VMEM((192, 2176), BF16)] * 2,
        compiler_params=PARAMS,
        cost_estimate=HINT if far else LONG,
    )(ids, stk, stk_other, og, og_other, pre, hid, recv)


def bump_kernel(x_up, x_down, y_up, y_down, a, b, c, d, *outs):
    for part, got, out in zip((x_up, x_down, y_up, y_down), (a, b, c, d), outs, strict=True):
        out[...] = (part[...].astype(F32) + got[...].astype(F32)).astype(BF16)


def bump_of(x_up, x_down, y_up, y_down, got):
    first = pl.BlockSpec((112, 2176), lambda i: (0, 0))
    second = pl.BlockSpec((112, 2176), lambda i: (1, 0))
    sides = [first, second, first, second]
    return pl.pallas_call(
        bump_kernel,
        out_shape=(struct((224, 2176), BF16),) * 4,
        grid=(1,),
        in_specs=sides + [first] * 4,
        out_specs=tuple(sides),
        input_output_aliases={0: 0, 1: 1, 2: 2, 3: 3},
        compiler_params=PARAMS,
        cost_estimate=HINT,
    )(x_up, x_down, y_up, y_down, *got)


def spread_kernel(where, a, b, c, *outs):
    value = (a[...].astype(F32) + b[...].astype(F32) + c[...].astype(F32)).astype(BF16)
    for n in range(4):
        piece = jnp.concatenate(
            [value[:, n * 320 : n * 320 + 320], value[:, 1280 + n * 224 : 1280 + n * 224 + 224]], axis=1
        )
        turn = lax.rem(n - where[0] + 4, 4)
        for k in range(4):

            @pl.when(turn == k)
            def _(k=k, piece=piece):
                outs[k][...] = piece


def spread_of(where, parts):
    return pl.pallas_call(
        spread_kernel,
        out_shape=(struct((224, 544), BF16),) * 4,
        in_specs=[SMEM] + [VMEM] * 3,
        out_specs=(VMEM,) * 4,
        compiler_params=PARAMS,
        cost_estimate=LONG,
    )(where, *parts)


def finish_kernel(a0, a1, a2, a3, b0, b1, b2, b3, grad_in, grad_out):
    first = a0[...].astype(F32) + a1[...].astype(F32) + a2[...].astype(F32) + a3[...].astype(F32)
    second = b0[...].astype(F32) + b1[...].astype(F32) + b2[...].astype(F32) + b3[...].astype(F32)
    both = jnp.concatenate([first, second], axis=0)
    grad_in[...] = both[:, 0:320].T.astype(BF16)
    grad_out[...] = both[:, 320:544].astype(BF16)


def finish_of(first, second):
    return pl.pallas_call(
        finish_kernel,
        out_shape=(struct((320, 448), BF16), struct((448, 224), BF16)),
        in_specs=[VMEM] * 8,
        out_specs=(VMEM, VMEM),
        compiler_params=PARAMS,
        cost_estimate=LONG,
    )(*first, *second)


def weight_sum_kernel(parts, out):
    total = parts[0].astype(F32)
    for k in range(1, 4):
        total = total + parts[k].astype(F32)
    out[...] = jnp.zeros_like(out)
    for n in range(16):
        out[n, 0:10, :] = total[n * 10 : n * 10 + 10].astype(BF16)


def weight_sum_of(parts):
    return pl.pallas_call(
        weight_sum_kernel,
        out_shape=struct((16, 16, 1280), BF16),
        in_specs=[VMEM],
        out_specs=VMEM,
        compiler_params=SMALL,
        cost_estimate=HINT,
    )(parts)


def ring_of(parts, shift):
    far = lax.ppermute(parts[2], "seq", shift(2))
    up = lax.ppermute(parts[1], "seq", shift(1))
    down = lax.ppermute(parts[3], "seq", shift(-1))
    return (parts[0], up, down, far)


def order_kernel(target, target_other, context, out, out_other):
    for where, to in ((target, out), (target_other, out_other)):
        pick = jnp.where(iota((1280, 128), 0) == where[...], 1.0, 0.0).astype(BF16)
        to[...] = mm(context[...], pick).T.astype(BF16)


def order_of(target, context):
    target = target.reshape(1, 1280)
    return pl.pallas_call(
        order_kernel,
        out_shape=(struct((640, 192), BF16),) * 2,
        grid=(5,),
        in_specs=[
            pl.BlockSpec((1, 128), lambda i: (0, i)),
            pl.BlockSpec((1, 128), lambda i: (0, i + 5)),
            whole((192, 1280)),
        ],
        out_specs=(pl.BlockSpec((128, 192), lambda i: (i, 0)),) * 2,
        compiler_params=SMALL,
        cost_estimate=LONG,
    )(target, target, context)


def out_weight_kernel(ctx, ctx_other, grad, grad_other, out):
    out[...] = (mm(ctx[...], grad[...]) + mm(ctx_other[...], grad_other[...])).astype(BF16)


def out_weight_of(ctx, ctx_other, grad, grad_other):
    block = pl.BlockSpec((192, 256), lambda i: (0, i))
    return pl.pallas_call(
        out_weight_kernel,
        out_shape=struct((640, 1280), BF16),
        grid=(5,),
        in_specs=[whole((640, 192)), whole((640, 192)), block, block],
        out_specs=pl.BlockSpec((640, 256), lambda i: (0, i)),
        compiler_params=SMALL,
        cost_estimate=HINT,
    )(ctx, ctx_other, grad, grad_other)


def swap(value):
    return lax.ppermute(value, "tp", CORE_SWAP)


def z_blocks(block):
    far = lax.ppermute(block, "tp", z_shift(2))
    behind = lax.ppermute(block, "tp", z_shift(1))
    ahead = lax.ppermute(block, "tp", z_shift(-1))
    return (block, ahead, far, behind)


def z_exchange(parts):
    return lax.all_to_all(parts, "tp", split_axis=0, concat_axis=0, axis_index_groups=Z_GROUPS, tiled=True)


def per_device(
    context,
    residual_in,
    out_weight,
    final_norm_weight,
    final_norm_bias,
    adapter_in,
    adapter_out,
    emb_grad,
    group_offsets,
    group_frames,
    group_owner,
):
    s = lax.axis_index("seq")
    t = lax.axis_index("tp")
    c = t % 2
    ids = jnp.stack([s // 4, s % 4, t // 2, c, s]).astype(jnp.int32)
    context = context.reshape(192, 1280)
    residual_in = residual_in.reshape(192, 1280)

    in_own = adapter_in.T
    in_other = swap(in_own)
    out_other = swap(adapter_out)

    parcels = parcels_of(ids, group_offsets, group_frames, group_owner, emb_grad.T)
    arrived = lax.all_to_all(parcels, "seq", split_axis=0, concat_axis=0, tiled=True)
    context, _ = lax.optimization_barrier((context, parcels))
    stacked_here, normed, inverse = encode_of(context, residual_in, out_weight, final_norm_weight, final_norm_bias)
    rows = z_blocks(stacked_here)
    arrived, in_other, out_other, _ = lax.optimization_barrier((arrived, in_other, out_other, stacked_here))

    keep, give = select_of(ids, group_owner, arrived)
    got = swap(give)
    grad_pair = pair_of(ids, keep, got)
    og = z_exchange(grad_pair)

    place = jnp.arange(1280, dtype=jnp.int32)
    core = (place // 640 + c) % 2
    target = (2 * ((place % 640) // 160) + core) * 10 + ((place % 160) // 10) * 80 + place % 10
    context_keep, context_give = order_of(target, context)
    context_got = swap(context_give)

    rows, _ = lax.optimization_barrier((rows, grad_pair))
    stk, hid_own, hid_other, slope_own, slope_other = preact_of(ids, rows, in_own, in_other)
    stk_other = swap(stk)
    og, _ = lax.optimization_barrier((og, context_give))
    og_other = swap(og)
    pre_own, send, pre_rows, pre_rows_other = pre_grad_of(
        og, adapter_out, out_other, hid_other, slope_own, slope_other
    )
    recv = swap(send)
    row_part = rows_of(pre_rows, pre_rows_other, in_own, in_other)
    row_parts = z_exchange(row_part.reshape(4, 48, 5120))

    pre_own, _ = lax.optimization_barrier((pre_own, row_part))
    operands = (ids, stk, stk_other, og, og_other, pre_own, hid_own, recv)
    x_far, x_far2, y_far, y_far2 = weight_grads_of(True, *operands)
    got = (
        lax.ppermute(x_far, "seq", x_shift(1)),
        lax.ppermute(x_far2, "seq", x_shift(-1)),
        lax.ppermute(y_far, "seq", y_shift(1)),
        lax.ppermute(y_far2, "seq", y_shift(-1)),
    )
    pre_own, _ = lax.optimization_barrier((pre_own, x_far))
    x_here, x_up, x_down, y_here, y_up, y_down = weight_grads_of(
        False, ids, stk, stk_other, og, og_other, pre_own, hid_own, recv
    )
    x_up, x_down, y_up, y_down = bump_of(x_up, x_down, y_up, y_down, got)
    row_parts, _ = lax.optimization_barrier((row_parts, x_up))

    d_residual = norm_back_of(row_parts, normed, inverse, final_norm_weight)
    residual_other = swap(d_residual)
    weight_part = out_weight_of(context_keep, context_got, d_residual, residual_other)
    residual_late, _ = lax.optimization_barrier((d_residual, weight_part))
    d_context = mm(residual_late, out_weight, 1, 1).astype(BF16)
    y_here, _ = lax.optimization_barrier((y_here, d_context))
    y_next = spread_of(
        ids[1:2], (y_here, lax.ppermute(y_up, "seq", y_shift(1)), lax.ppermute(y_down, "seq", y_shift(-1)))
    )
    x_sums = (x_here, lax.ppermute(x_up, "seq", x_shift(1)), lax.ppermute(x_down, "seq", x_shift(-1)))

    weight_parts, _ = lax.optimization_barrier((z_exchange(weight_part.reshape(4, 160, 1280)), y_next[0]))
    weight_z = weight_sum_of(weight_parts)
    pieces = lax.all_to_all(weight_z, "seq", split_axis=0, concat_axis=0, tiled=True)
    d_out_weight = jnp.sum(pieces.astype(F32), axis=0)[:10]

    x_next = spread_of(ids[0:1], x_sums)
    first = ring_of(x_next, y_shift)
    second = ring_of(y_next, x_shift)
    grad_in, grad_out = finish_of(first, second)

    return (
        d_context.reshape(8, 24, 1280),
        d_residual.reshape(8, 24, 1280),
        d_out_weight,
        grad_in,
        grad_out,
    )


def solution(mesh):
    placed = (
        P("seq", "tp", None),
        P("seq", "tp", None),
        P(),
        P(),
        P(),
        P(None, "tp"),
        P("tp", None),
        P("seq", "tp"),
        P(),
        P(),
        P(),
    )
    return jax.shard_map(
        per_device,
        mesh=mesh,
        in_specs=placed,
        out_specs=(
            P("seq", "tp", None),
            P("seq", "tp", None),
            P(("seq", "tp"), None),
            P("seq", "tp"),
            P("tp", "seq"),
        ),
        check_vma=False,
    )
```

```python
import jax
import jax.numpy as jnp
from jax import lax
from jax.experimental import pallas as pl
from jax.experimental.pallas import tpu as pltpu
from jax.sharding import PartitionSpec as P

F32 = jnp.float32
BF16 = jnp.bfloat16
ZN, CN = 4, 2
YN, XN = 4, 4
TP = ZN * CN
PARAMS = pltpu.CompilerParams(vmem_limit_bytes=56 * 1024 * 1024)
SMALL = pltpu.CompilerParams(vmem_limit_bytes=20 * 1024 * 1024)

CORE_SWAP = [(i, i ^ 1) for i in range(TP)]
Z_GROUPS = [[z * CN + c for z in range(ZN)] for c in range(CN)]


def z_shift(step):
    return [(z * CN + c, ((z + step) % ZN) * CN + c) for z in range(ZN) for c in range(CN)]


def x_shift(step):
    return [(y * XN + x, y * XN + (x + step) % XN) for y in range(YN) for x in range(XN)]


def y_shift(step):
    return [(y * XN + x, ((y + step) % YN) * XN + x) for y in range(YN) for x in range(XN)]


def gelu_parts(values):
    cumulative = 0.5 * (1.0 + lax.erf(values * 0.7071067811865476))
    density = jnp.exp(-0.5 * values * values) * 0.3989422804014327
    return values * cumulative, cumulative + values * density


def mm(a, b, ca=1, cb=0):
    return lax.dot_general(a, b, (((ca,), (cb,)), ((), ())), preferred_element_type=F32)


def iota(shape, dim):
    return lax.broadcasted_iota(jnp.int32, shape, dim)


def struct(shape, dtype):
    return jax.ShapeDtypeStruct(shape, dtype)


def whole(shape):
    return pl.BlockSpec(shape, lambda *_: (0,) * len(shape))


SMEM = pl.BlockSpec(memory_space=pltpu.SMEM)
VMEM = pl.BlockSpec(memory_space=pltpu.VMEM)


HINT = pl.CostEstimate(flops=1, bytes_accessed=1, transcendentals=0)
LONG = pl.CostEstimate(flops=40_000_000_000, bytes_accessed=100_000_000, transcendentals=1_000_000)


def parcel_kernel(ids, offsets, frames, owner, grad_t, out):
    out[...] = jnp.zeros_like(out)
    s = ids[4]
    row, col = iota((48, 384), 0), iota((48, 384), 1)
    picks, dests = [], []
    for k in range(8):
        group = s * 8 + k
        start = offsets[group] - s * 384
        count = lax.shift_right_logical(frames[group], 2)
        dests.append(lax.shift_right_logical(owner[group], 3))
        picks.append(jnp.where((row < count) & (col == row + start), 1.0, 0.0))
    tokens = mm(jnp.concatenate(picks).astype(BF16), grad_t[...], 1, 1).astype(BF16)
    for k in range(8):
        out[dests[k]] = tokens[k * 48 : k * 48 + 48]


def parcels_of(ids, offsets, frames, owner, grad_t):
    return pl.pallas_call(
        parcel_kernel,
        out_shape=struct((16, 48, 448), BF16),
        in_specs=[SMEM, SMEM, SMEM, SMEM, VMEM],
        out_specs=VMEM,
        compiler_params=PARAMS,
        cost_estimate=HINT,
    )(ids, offsets, frames, owner, grad_t)


def select_kernel(ids, owner, arrived, keep, give):
    s, c = ids[4], ids[3]
    row = iota((192, 128), 0)
    z = lax.shift_right_logical(row * 1366, 16)
    rest = row - z * 48
    slot = lax.shift_right_logical(rest * 10923, 16)
    six = rest - slot * 6
    group = iota((192, 128), 1)
    source = jnp.sum(
        jnp.where(owner[...] == s * 8 + slot, lax.shift_right_logical(group, 3), 0), axis=1, keepdims=True
    )
    column = iota((192, 768), 1)
    tokens = arrived[...].reshape(768, 448)
    base = source * 48 + z[:, :1] * 12 + six[:, :1]
    for out, core in ((keep, c), (give, 1 - c)):
        route = jnp.where(column == base + core * 6, 1.0, 0.0).astype(BF16)
        out[...] = mm(route, tokens).astype(BF16)


def select_of(ids, owner, arrived):
    return pl.pallas_call(
        select_kernel,
        out_shape=(struct((192, 448), BF16), struct((192, 448), BF16)),
        in_specs=[SMEM, VMEM, VMEM],
        out_specs=(VMEM, VMEM),
        compiler_params=PARAMS,
        cost_estimate=HINT,
    )(ids, owner.reshape(1, 128), arrived)


def pair_kernel(ids, keep, got, out):
    first = ids[3] == 0
    both = jnp.concatenate(
        [jnp.where(first, keep[...], got[...]), jnp.where(first, got[...], keep[...])], axis=1
    )
    for k in range(4):
        out[k] = both


def pair_of(ids, keep, got):
    return pl.pallas_call(
        pair_kernel,
        out_shape=struct((4, 192, 896), BF16),
        in_specs=[SMEM, VMEM, VMEM],
        out_specs=VMEM,
        compiler_params=PARAMS,
        cost_estimate=HINT,
    )(ids, keep, got)


def encode_kernel(context, residual, weight, gain, bias, stacked, normed, inverse, scratch):
    stream = residual[...].astype(F32) + mm(context[...], weight[...])
    centered = stream - jnp.mean(stream, axis=-1, keepdims=True)
    inv = lax.rsqrt(jnp.mean(centered * centered, axis=-1, keepdims=True) + 1e-05)
    norm = centered * inv
    normed[...] = norm
    inverse[...] = jnp.broadcast_to(inv, inverse.shape)
    encoded = norm * gain[...] + bias[...]
    for piece in range(10):
        scratch[piece] = encoded[:, piece * 128 : (piece + 1) * 128]
    for r in range(4):
        for piece in range(10):
            at = r * 1280 + piece * 128
            stacked[:, at : at + 128] = scratch[piece, pl.ds(r, 48, stride=4), :].astype(BF16)


def encode_of(context, residual, weight, gain, bias):
    return pl.pallas_call(
        encode_kernel,
        out_shape=(struct((48, 5120), BF16), struct((192, 1280), F32), struct((192, 128), F32)),
        in_specs=[VMEM] * 5,
        out_specs=(VMEM,) * 3,
        scratch_shapes=[pltpu.VMEM((10, 192, 128), F32)],
        compiler_params=PARAMS,
        cost_estimate=HINT,
    )(context, residual, weight, gain.reshape(1, 1280), bias.reshape(1, 1280))


def norm_back_kernel(rows, normed, inverse, gain, out, scratch):
    for r in range(4):
        for piece in range(10):
            at = r * 1280 + piece * 128
            total = rows[0, :, at : at + 128].astype(F32)
            for k in range(1, 4):
                total = total + rows[k, :, at : at + 128].astype(F32)
            scratch[piece, pl.ds(r, 48, stride=4), :] = total.astype(BF16).astype(F32)
    scaled = jnp.concatenate([scratch[piece] for piece in range(10)], axis=1) * gain[...]
    norm = normed[...]
    mean = jnp.mean(scaled, axis=-1, keepdims=True)
    along = jnp.mean(scaled * norm, axis=-1, keepdims=True)
    out[...] = (inverse[:, :1] * (scaled - mean - norm * along)).astype(BF16)


def norm_back_of(rows, normed, inverse, gain):
    return pl.pallas_call(
        norm_back_kernel,
        out_shape=struct((192, 1280), BF16),
        in_specs=[VMEM] * 4,
        out_specs=VMEM,
        scratch_shapes=[pltpu.VMEM((10, 192, 128), F32)],
        compiler_params=SMALL,
        cost_estimate=LONG,
    )(rows, normed, inverse, gain.reshape(1, 1280))


def preact_kernel(ids, b0, b1, b2, b3, own_w, other_w, stk, hid_own, hid_other, slope_own, slope_other, acc, acc_other):
    i = pl.program_id(0)
    for step, block in enumerate((b0, b1, b2, b3)):
        at = pl.multiple_of(lax.rem(ids[2] + step, 4) * 48, 16)
        stk[pl.ds(at, 48), :] = block[...]

    @pl.when(i == 0)
    def _():
        acc[...] = jnp.zeros_like(acc)
        acc_other[...] = jnp.zeros_like(acc_other)

    rows = stk[...]
    acc[...] += mm(own_w[...], rows, 1, 1)
    acc_other[...] += mm(other_w[...], rows, 1, 1)

    @pl.when(i == pl.num_programs(0) - 1)
    def _():
        hidden, slope = gelu_parts(acc[...])
        hid_own[...] = hidden.astype(BF16)
        slope_own[...] = slope
        hidden, slope = gelu_parts(acc_other[...])
        hid_other[...] = hidden.astype(BF16)
        slope_other[...] = slope


def preact_of(ids, blocks, own_w, other_w):
    return pl.pallas_call(
        preact_kernel,
        out_shape=(
            struct((192, 5120), BF16),
            struct((448, 192), BF16),
            struct((448, 192), BF16),
            struct((448, 192), F32),
            struct((448, 192), F32),
        ),
        grid=(5,),
        in_specs=[SMEM]
        + [pl.BlockSpec((48, 1024), lambda i: (0, i))] * 4
        + [pl.BlockSpec((448, 1024), lambda i: (0, i))] * 2,
        out_specs=(pl.BlockSpec((192, 1024), lambda i: (0, i)),) + (whole((448, 192)),) * 4,
        scratch_shapes=[pltpu.VMEM((448, 192), F32)] * 2,
        compiler_params=PARAMS,
        cost_estimate=HINT,
    )(ids, *blocks, own_w, other_w)


def pre_grad_kernel(
    og, out_own, out_other, in_own, in_other, hid_other, slope_own, slope_other,
    row_part, pre_own, send, out_w, in_w, og_w, slope_w, row_w, out_sem, in_sem, og_sem, slope_sem, row_sem,
):
    copy = pltpu.make_async_copy

    def load(source, to, sem, w, j, width):
        at = pl.ds(j * width, width)
        return copy(source.at[:, at], to.at[w, :, at], sem.at[w, j])

    outs, ins = (out_own, out_other), (in_own, in_other)
    pieces = [copy(og.at[j], og_w.at[j], og_sem.at[j]) for j in range(4)]
    slopes = [copy(ref, slope_w.at[w], slope_sem.at[w]) for w, ref in enumerate((slope_own, slope_other))]
    queue = [[pieces[j]] + [load(outs[w], out_w, out_sem, w, j, 896) for w in range(2)] for j in range(4)]
    queue[3] += slopes
    queue += [[load(ins[w], in_w, in_sem, w, j, 1280) for w in range(2)] for j in range(4)]

    def begin(n):
        if n < len(queue):
            for part in queue[n]:
                part.start()

    def arrive(n):
        for part in queue[n]:
            part.wait()
        begin(n + 4)

    for n in range(4):
        begin(n)
    sums = [jnp.zeros((448, 192), F32)] * 2
    for j in range(4):
        arrive(j)
        for w in range(2):
            sums[w] = sums[w] + mm(out_w[w, :, j * 896 : j * 896 + 896], og_w[j], 1, 1)
    own = sums[0] * slope_w[0]
    other = sums[1] * slope_w[1]
    pre_own[...] = own.astype(BF16)
    send[0:448, :] = other.astype(BF16)
    send[448:896, :] = hid_other[...]
    turned = (own.T.astype(BF16), other.T.astype(BF16))
    stores = []
    for j in range(4):
        arrive(4 + j)
        at = slice(j * 1280, j * 1280 + 1280)
        row_w[:, at] = (mm(turned[0], in_w[0, :, at]) + mm(turned[1], in_w[1, :, at])).astype(BF16)
        span = pl.ds(j * 1280, 1280)
        stores.append(copy(row_w.at[:, span], row_part.at[:, span], row_sem.at[j]))
        stores[-1].start()
    for store in stores:
        store.wait()


def pre_grad_of(og, out_own, out_other, in_own, in_other, hid_other, slope_own, slope_other):
    held = pl.BlockSpec(memory_space=pl.ANY)
    return pl.pallas_call(
        pre_grad_kernel,
        out_shape=(struct((192, 5120), BF16), struct((448, 192), BF16), struct((896, 192), BF16)),
        in_specs=[held] * 5 + [VMEM, held, held],
        out_specs=(held, VMEM, VMEM),
        scratch_shapes=[
            pltpu.VMEM((2, 448, 3584), BF16),
            pltpu.VMEM((2, 448, 5120), BF16),
            pltpu.VMEM((4, 192, 896), BF16),
            pltpu.VMEM((2, 448, 192), F32),
            pltpu.VMEM((192, 5120), BF16),
            pltpu.SemaphoreType.DMA((2, 4)),
            pltpu.SemaphoreType.DMA((2, 4)),
            pltpu.SemaphoreType.DMA((4,)),
            pltpu.SemaphoreType.DMA((2,)),
            pltpu.SemaphoreType.DMA((4,)),
        ],
        compiler_params=PARAMS,
        cost_estimate=HINT,
    )(og, out_own, out_other, in_own, in_other, hid_other, slope_own, slope_other)


def x_columns(stk, og, x, out):
    for y in range(4):
        out[:, y * 320 : y * 320 + 320] = stk[:, (4 * y + x) * 320 : (4 * y + x + 1) * 320]
        out[:, 1280 + y * 224 : 1504 + y * 224] = og[y, :, x * 224 : x * 224 + 224]


def weight_grad_kernel(far, ids, stk, stk_other, og, og_other, pre, hid, recv, *outs):
    i = pl.program_id(0)
    turn = 2 if far else jnp.where(i == 2, 3, i)
    x_at, y_at = lax.rem(ids[1] + turn, 4), lax.rem(ids[0] + turn, 4)
    picked, picked_other = outs[-2:]
    for x in range(4):

        @pl.when(x_at == x)
        def _(x=x):
            x_columns(stk, og, x, picked)
            x_columns(stk_other, og_other, x, picked_other)

    across = jnp.concatenate(
        [
            mm(pre[0:224], picked[:, 0:1280]) + mm(recv[0:224], picked_other[:, 0:1280]),
            mm(hid[0:224], picked[:, 1280:2176]) + mm(recv[448:672], picked_other[:, 1280:2176]),
        ],
        axis=1,
    ).astype(BF16)
    at = pl.ds(pl.multiple_of(y_at * 1280, 128), 1280)
    down = jnp.concatenate(
        [
            mm(pre[224:448], stk[:, at]) + mm(recv[224:448], stk_other[:, at]),
            mm(hid[224:448], og[y_at]) + mm(recv[672:896], og_other[y_at]),
        ],
        axis=1,
    ).astype(BF16)
    if far:
        outs[0][...] = across[0:112]
        outs[1][...] = across[112:224]
        outs[2][...] = down[0:112]
        outs[3][...] = down[112:224]
        return
    for k in range(3):

        @pl.when(i == k)
        def _(k=k):
            outs[k][...] = across
            outs[3 + k][...] = down


def weight_grads_of(far, ids, stk, stk_other, og, og_other, pre, hid, recv):
    once = pl.Buffered(buffer_count=1)

    def single(shape):
        return pl.BlockSpec(shape, lambda *_: (0,) * len(shape), pipeline_mode=once)

    def kernel(*refs):
        weight_grad_kernel(far, *refs)

    shapes = [(112, 2176)] * 4 if far else [(224, 2176)] * 6
    return pl.pallas_call(
        kernel,
        out_shape=tuple(struct(shape, BF16) for shape in shapes),
        grid=(1 if far else 3,),
        in_specs=[SMEM]
        + [single((192, 5120))] * 2
        + [single((4, 192, 896))] * 2
        + [single((448, 192)), single((448, 192)), single((896, 192))],
        out_specs=tuple(single(shape) for shape in shapes),
        scratch_shapes=[pltpu.VMEM((192, 2176), BF16)] * 2,
        compiler_params=PARAMS,
        cost_estimate=HINT if far else LONG,
    )(ids, stk, stk_other, og, og_other, pre, hid, recv)


def bump_kernel(x_up, x_down, y_up, y_down, a, b, c, d, *outs):
    for part, got, out in zip((x_up, x_down, y_up, y_down), (a, b, c, d), outs, strict=True):
        out[...] = (part[...].astype(F32) + got[...].astype(F32)).astype(BF16)


def bump_of(x_up, x_down, y_up, y_down, got):
    first = pl.BlockSpec((112, 2176), lambda i: (0, 0))
    second = pl.BlockSpec((112, 2176), lambda i: (1, 0))
    sides = [first, second, first, second]
    return pl.pallas_call(
        bump_kernel,
        out_shape=(struct((224, 2176), BF16),) * 4,
        grid=(1,),
        in_specs=sides + [first] * 4,
        out_specs=tuple(sides),
        input_output_aliases={0: 0, 1: 1, 2: 2, 3: 3},
        compiler_params=PARAMS,
        cost_estimate=HINT,
    )(x_up, x_down, y_up, y_down, *got)


def spread_kernel(where, a, b, c, *outs):
    value = (a[...].astype(F32) + b[...].astype(F32) + c[...].astype(F32)).astype(BF16)
    for n in range(4):
        piece = jnp.concatenate(
            [value[:, n * 320 : n * 320 + 320], value[:, 1280 + n * 224 : 1280 + n * 224 + 224]], axis=1
        )
        turn = lax.rem(n - where[0] + 4, 4)
        for k in range(4):

            @pl.when(turn == k)
            def _(k=k, piece=piece):
                outs[k][...] = piece


def spread_of(where, parts):
    return pl.pallas_call(
        spread_kernel,
        out_shape=(struct((224, 544), BF16),) * 4,
        in_specs=[SMEM] + [VMEM] * 3,
        out_specs=(VMEM,) * 4,
        compiler_params=PARAMS,
        cost_estimate=LONG,
    )(where, *parts)


def finish_kernel(a0, a1, a2, a3, b0, b1, b2, b3, grad_in, grad_out):
    first = a0[...].astype(F32) + a1[...].astype(F32) + a2[...].astype(F32) + a3[...].astype(F32)
    second = b0[...].astype(F32) + b1[...].astype(F32) + b2[...].astype(F32) + b3[...].astype(F32)
    both = jnp.concatenate([first, second], axis=0)
    grad_in[...] = both[:, 0:320].T.astype(BF16)
    grad_out[...] = both[:, 320:544].astype(BF16)


def finish_of(first, second):
    return pl.pallas_call(
        finish_kernel,
        out_shape=(struct((320, 448), BF16), struct((448, 224), BF16)),
        in_specs=[VMEM] * 8,
        out_specs=(VMEM, VMEM),
        compiler_params=PARAMS,
        cost_estimate=LONG,
    )(*first, *second)


def weight_sum_kernel(parts, out):
    total = parts[0].astype(F32)
    for k in range(1, 4):
        total = total + parts[k].astype(F32)
    out[...] = jnp.zeros_like(out)
    for n in range(16):
        out[n, 0:10, :] = total[n * 10 : n * 10 + 10].astype(BF16)


def weight_sum_of(parts):
    return pl.pallas_call(
        weight_sum_kernel,
        out_shape=struct((16, 16, 1280), BF16),
        in_specs=[VMEM],
        out_specs=VMEM,
        compiler_params=SMALL,
        cost_estimate=HINT,
    )(parts)


def ring_of(parts, shift):
    far = lax.ppermute(parts[2], "seq", shift(2))
    up = lax.ppermute(parts[1], "seq", shift(1))
    down = lax.ppermute(parts[3], "seq", shift(-1))
    return (parts[0], up, down, far)


def order_kernel(target, target_other, context, out, out_other):
    for where, to in ((target, out), (target_other, out_other)):
        pick = jnp.where(iota((1280, 128), 0) == where[...], 1.0, 0.0).astype(BF16)
        to[...] = mm(context[...], pick).T.astype(BF16)


def order_of(target, context):
    target = target.reshape(1, 1280)
    return pl.pallas_call(
        order_kernel,
        out_shape=(struct((640, 192), BF16),) * 2,
        grid=(5,),
        in_specs=[
            pl.BlockSpec((1, 128), lambda i: (0, i)),
            pl.BlockSpec((1, 128), lambda i: (0, i + 5)),
            whole((192, 1280)),
        ],
        out_specs=(pl.BlockSpec((128, 192), lambda i: (i, 0)),) * 2,
        compiler_params=SMALL,
        cost_estimate=LONG,
    )(target, target, context)


def out_weight_kernel(ctx, ctx_other, grad, grad_other, out):
    out[...] = (mm(ctx[...], grad[...]) + mm(ctx_other[...], grad_other[...])).astype(BF16)


def out_weight_of(ctx, ctx_other, grad, grad_other):
    block = pl.BlockSpec((192, 256), lambda i: (0, i))
    return pl.pallas_call(
        out_weight_kernel,
        out_shape=struct((640, 1280), BF16),
        grid=(5,),
        in_specs=[whole((640, 192)), whole((640, 192)), block, block],
        out_specs=pl.BlockSpec((640, 256), lambda i: (0, i)),
        compiler_params=SMALL,
        cost_estimate=HINT,
    )(ctx, ctx_other, grad, grad_other)


def swap(value):
    return lax.ppermute(value, "tp", CORE_SWAP)


def z_blocks(block):
    far = lax.ppermute(block, "tp", z_shift(2))
    behind = lax.ppermute(block, "tp", z_shift(1))
    ahead = lax.ppermute(block, "tp", z_shift(-1))
    return (block, ahead, far, behind)


def z_exchange(parts):
    return lax.all_to_all(parts, "tp", split_axis=0, concat_axis=0, axis_index_groups=Z_GROUPS, tiled=True)


def per_device(
    context,
    residual_in,
    out_weight,
    final_norm_weight,
    final_norm_bias,
    adapter_in,
    adapter_out,
    emb_grad,
    group_offsets,
    group_frames,
    group_owner,
):
    s = lax.axis_index("seq")
    t = lax.axis_index("tp")
    c = t % 2
    ids = jnp.stack([s // 4, s % 4, t // 2, c, s]).astype(jnp.int32)
    context = context.reshape(192, 1280)
    residual_in = residual_in.reshape(192, 1280)

    in_own = adapter_in.T
    in_other = swap(in_own)
    out_other = swap(adapter_out)

    parcels = parcels_of(ids, group_offsets, group_frames, group_owner, emb_grad.T)
    arrived = lax.all_to_all(parcels, "seq", split_axis=0, concat_axis=0, tiled=True)
    context, _ = lax.optimization_barrier((context, parcels))
    stacked_here, normed, inverse = encode_of(context, residual_in, out_weight, final_norm_weight, final_norm_bias)
    rows = z_blocks(stacked_here)
    arrived, in_other, out_other, _ = lax.optimization_barrier((arrived, in_other, out_other, stacked_here))

    keep, give = select_of(ids, group_owner, arrived)
    got = swap(give)
    grad_pair = pair_of(ids, keep, got)
    og = z_exchange(grad_pair)

    place = jnp.arange(1280, dtype=jnp.int32)
    core = (place // 640 + c) % 2
    target = (2 * ((place % 640) // 160) + core) * 10 + ((place % 160) // 10) * 80 + place % 10
    context_keep, context_give = order_of(target, context)
    context_got = swap(context_give)

    rows, _ = lax.optimization_barrier((rows, grad_pair))
    stk, hid_own, hid_other, slope_own, slope_other = preact_of(ids, rows, in_own, in_other)
    stk_other = swap(stk)
    og, _ = lax.optimization_barrier((og, context_give))
    og_other = swap(og)
    row_part, pre_own, send = pre_grad_of(
        og, adapter_out, out_other, in_own, in_other, hid_other, slope_own, slope_other
    )
    recv = swap(send)
    row_parts = z_exchange(row_part.reshape(4, 48, 5120))

    pre_own, _ = lax.optimization_barrier((pre_own, row_part))
    operands = (ids, stk, stk_other, og, og_other, pre_own, hid_own, recv)
    x_far, x_far2, y_far, y_far2 = weight_grads_of(True, *operands)
    got = (
        lax.ppermute(x_far, "seq", x_shift(1)),
        lax.ppermute(x_far2, "seq", x_shift(-1)),
        lax.ppermute(y_far, "seq", y_shift(1)),
        lax.ppermute(y_far2, "seq", y_shift(-1)),
    )
    pre_own, _ = lax.optimization_barrier((pre_own, x_far))
    x_here, x_up, x_down, y_here, y_up, y_down = weight_grads_of(
        False, ids, stk, stk_other, og, og_other, pre_own, hid_own, recv
    )
    x_up, x_down, y_up, y_down = bump_of(x_up, x_down, y_up, y_down, got)
    row_parts, _ = lax.optimization_barrier((row_parts, x_up))

    d_residual = norm_back_of(row_parts, normed, inverse, final_norm_weight)
    residual_other = swap(d_residual)
    weight_part = out_weight_of(context_keep, context_got, d_residual, residual_other)
    residual_late, _ = lax.optimization_barrier((d_residual, weight_part))
    d_context = mm(residual_late, out_weight, 1, 1).astype(BF16)
    y_here, _ = lax.optimization_barrier((y_here, d_context))
    y_next = spread_of(
        ids[1:2], (y_here, lax.ppermute(y_up, "seq", y_shift(1)), lax.ppermute(y_down, "seq", y_shift(-1)))
    )
    x_sums = (x_here, lax.ppermute(x_up, "seq", x_shift(1)), lax.ppermute(x_down, "seq", x_shift(-1)))

    weight_parts, _ = lax.optimization_barrier((z_exchange(weight_part.reshape(4, 160, 1280)), y_next[0]))
    weight_z = weight_sum_of(weight_parts)
    pieces = lax.all_to_all(weight_z, "seq", split_axis=0, concat_axis=0, tiled=True)
    d_out_weight = jnp.sum(pieces.astype(F32), axis=0)[:10]

    x_next = spread_of(ids[0:1], x_sums)
    first = ring_of(x_next, y_shift)
    second = ring_of(y_next, x_shift)
    grad_in, grad_out = finish_of(first, second)

    return (
        d_context.reshape(8, 24, 1280),
        d_residual.reshape(8, 24, 1280),
        d_out_weight,
        grad_in,
        grad_out,
    )


def solution(mesh):
    placed = (
        P("seq", "tp", None),
        P("seq", "tp", None),
        P(),
        P(),
        P(),
        P(None, "tp"),
        P("tp", None),
        P("seq", "tp"),
        P(),
        P(),
        P(),
    )
    return jax.shard_map(
        per_device,
        mesh=mesh,
        in_specs=placed,
        out_specs=(
            P("seq", "tp", None),
            P("seq", "tp", None),
            P(("seq", "tp"), None),
            P("seq", "tp"),
            P("tp", "seq"),
        ),
        check_vma=False,
    )
```

```python
import jax
import jax.numpy as jnp
from jax import lax
from jax.experimental import pallas as pl
from jax.experimental.pallas import tpu as pltpu
from jax.sharding import PartitionSpec as P

F32 = jnp.float32
BF16 = jnp.bfloat16
ZN, CN = 4, 2
YN, XN = 4, 4
TP = ZN * CN
PARAMS = pltpu.CompilerParams(vmem_limit_bytes=56 * 1024 * 1024)
SMALL = pltpu.CompilerParams(vmem_limit_bytes=20 * 1024 * 1024)

CORE_SWAP = [(i, i ^ 1) for i in range(TP)]
Z_GROUPS = [[z * CN + c for z in range(ZN)] for c in range(CN)]


def z_shift(step):
    return [(z * CN + c, ((z + step) % ZN) * CN + c) for z in range(ZN) for c in range(CN)]


def x_shift(step):
    return [(y * XN + x, y * XN + (x + step) % XN) for y in range(YN) for x in range(XN)]


def y_shift(step):
    return [(y * XN + x, ((y + step) % YN) * XN + x) for y in range(YN) for x in range(XN)]


def gelu_parts(values):
    cumulative = 0.5 * (1.0 + lax.erf(values * 0.7071067811865476))
    density = jnp.exp(-0.5 * values * values) * 0.3989422804014327
    return values * cumulative, cumulative + values * density


def mm(a, b, ca=1, cb=0):
    return lax.dot_general(a, b, (((ca,), (cb,)), ((), ())), preferred_element_type=F32)


def iota(shape, dim):
    return lax.broadcasted_iota(jnp.int32, shape, dim)


def struct(shape, dtype):
    return jax.ShapeDtypeStruct(shape, dtype)


def whole(shape):
    return pl.BlockSpec(shape, lambda *_: (0,) * len(shape))


SMEM = pl.BlockSpec(memory_space=pltpu.SMEM)
VMEM = pl.BlockSpec(memory_space=pltpu.VMEM)


HINT = pl.CostEstimate(flops=1, bytes_accessed=1, transcendentals=0)
LONG = pl.CostEstimate(flops=40_000_000_000, bytes_accessed=100_000_000, transcendentals=1_000_000)


def parcel_kernel(offsets, frames, owner, grad_t, out):
    out[...] = jnp.zeros_like(out)
    s = lax.axis_index("seq")
    row, col = iota((48, 384), 0), iota((48, 384), 1)
    picks, dests = [], []
    for k in range(8):
        group = s * 8 + k
        start = offsets[group] - s * 384
        count = lax.shift_right_logical(frames[group], 2)
        dests.append(lax.shift_right_logical(owner[group], 3))
        picks.append(jnp.where((row < count) & (col == row + start), 1.0, 0.0))
    tokens = mm(jnp.concatenate(picks).astype(BF16), grad_t[...], 1, 1).astype(BF16)
    for k in range(8):
        out[dests[k]] = tokens[k * 48 : k * 48 + 48]


def parcels_of(offsets, frames, owner, grad_t):
    return pl.pallas_call(
        parcel_kernel,
        out_shape=struct((16, 48, 448), BF16),
        in_specs=[SMEM, SMEM, SMEM, VMEM],
        out_specs=VMEM,
        compiler_params=PARAMS,
        cost_estimate=HINT,
    )(offsets, frames, owner, grad_t)


def select_kernel(ids, owner, arrived, keep, give):
    s, c = ids[4], ids[3]
    row = iota((192, 128), 0)
    z = lax.shift_right_logical(row * 1366, 16)
    rest = row - z * 48
    slot = lax.shift_right_logical(rest * 10923, 16)
    six = rest - slot * 6
    group = iota((192, 128), 1)
    source = jnp.sum(
        jnp.where(owner[...] == s * 8 + slot, lax.shift_right_logical(group, 3), 0), axis=1, keepdims=True
    )
    column = iota((192, 768), 1)
    tokens = arrived[...].reshape(768, 448)
    base = source * 48 + z[:, :1] * 12 + six[:, :1]
    for out, core in ((keep, c), (give, 1 - c)):
        route = jnp.where(column == base + core * 6, 1.0, 0.0).astype(BF16)
        out[...] = mm(route, tokens).astype(BF16)


def select_of(ids, owner, arrived):
    return pl.pallas_call(
        select_kernel,
        out_shape=(struct((192, 448), BF16), struct((192, 448), BF16)),
        in_specs=[SMEM, VMEM, VMEM],
        out_specs=(VMEM, VMEM),
        compiler_params=PARAMS,
        cost_estimate=HINT,
    )(ids, owner.reshape(1, 128), arrived)


def pair_kernel(ids, keep, got, out):
    first = ids[3] == 0
    both = jnp.concatenate(
        [jnp.where(first, keep[...], got[...]), jnp.where(first, got[...], keep[...])], axis=1
    )
    for k in range(4):
        out[k] = both


def pair_of(ids, keep, got):
    return pl.pallas_call(
        pair_kernel,
        out_shape=struct((4, 192, 896), BF16),
        in_specs=[SMEM, VMEM, VMEM],
        out_specs=VMEM,
        compiler_params=PARAMS,
        cost_estimate=HINT,
    )(ids, keep, got)


def encode_kernel(context, residual, weight, gain, bias, stacked, normed, inverse, scratch):
    stream = residual[...].astype(F32) + mm(context[...], weight[...])
    centered = stream - jnp.mean(stream, axis=-1, keepdims=True)
    inv = lax.rsqrt(jnp.mean(centered * centered, axis=-1, keepdims=True) + 1e-05)
    norm = centered * inv
    normed[...] = norm
    inverse[...] = jnp.broadcast_to(inv, inverse.shape)
    encoded = norm * gain[...] + bias[...]
    for piece in range(10):
        scratch[piece] = encoded[:, piece * 128 : (piece + 1) * 128]
    for r in range(4):
        for piece in range(10):
            at = r * 1280 + piece * 128
            stacked[:, at : at + 128] = scratch[piece, pl.ds(r, 48, stride=4), :].astype(BF16)


def encode_of(context, residual, weight, gain, bias):
    return pl.pallas_call(
        encode_kernel,
        out_shape=(struct((48, 5120), BF16), struct((192, 1280), F32), struct((192, 128), F32)),
        in_specs=[VMEM] * 5,
        out_specs=(VMEM,) * 3,
        scratch_shapes=[pltpu.VMEM((10, 192, 128), F32)],
        compiler_params=PARAMS,
        cost_estimate=HINT,
    )(context, residual, weight, gain.reshape(1, 1280), bias.reshape(1, 1280))


def norm_back_kernel(rows, normed, inverse, gain, out, scratch):
    for r in range(4):
        for piece in range(10):
            at = r * 1280 + piece * 128
            total = rows[0, :, at : at + 128].astype(F32)
            for k in range(1, 4):
                total = total + rows[k, :, at : at + 128].astype(F32)
            scratch[piece, pl.ds(r, 48, stride=4), :] = total.astype(BF16).astype(F32)
    scaled = jnp.concatenate([scratch[piece] for piece in range(10)], axis=1) * gain[...]
    norm = normed[...]
    mean = jnp.mean(scaled, axis=-1, keepdims=True)
    along = jnp.mean(scaled * norm, axis=-1, keepdims=True)
    out[...] = (inverse[:, :1] * (scaled - mean - norm * along)).astype(BF16)


def norm_back_of(rows, normed, inverse, gain):
    return pl.pallas_call(
        norm_back_kernel,
        out_shape=struct((192, 1280), BF16),
        in_specs=[VMEM] * 4,
        out_specs=VMEM,
        scratch_shapes=[pltpu.VMEM((10, 192, 128), F32)],
        compiler_params=SMALL,
        cost_estimate=LONG,
    )(rows, normed, inverse, gain.reshape(1, 1280))


def preact_kernel(ids, b0, b1, b2, b3, own_w, other_w, stk, hid_own, hid_other, slope_own, slope_other, acc, acc_other):
    i = pl.program_id(0)
    for step, block in enumerate((b0, b1, b2, b3)):
        at = pl.multiple_of(lax.rem(ids[2] + step, 4) * 48, 16)
        stk[pl.ds(at, 48), :] = block[...]

    @pl.when(i == 0)
    def _():
        acc[...] = jnp.zeros_like(acc)
        acc_other[...] = jnp.zeros_like(acc_other)

    rows = stk[...]
    acc[...] += mm(own_w[...], rows, 1, 1)
    acc_other[...] += mm(other_w[...], rows, 1, 1)

    @pl.when(i == pl.num_programs(0) - 1)
    def _():
        hidden, slope = gelu_parts(acc[...])
        hid_own[...] = hidden.astype(BF16)
        slope_own[...] = slope
        hidden, slope = gelu_parts(acc_other[...])
        hid_other[...] = hidden.astype(BF16)
        slope_other[...] = slope


def preact_of(ids, blocks, own_w, other_w):
    return pl.pallas_call(
        preact_kernel,
        out_shape=(
            struct((192, 5120), BF16),
            struct((448, 192), BF16),
            struct((448, 192), BF16),
            struct((448, 192), F32),
            struct((448, 192), F32),
        ),
        grid=(2,),
        in_specs=[SMEM]
        + [pl.BlockSpec((48, 2560), lambda i: (0, i))] * 4
        + [pl.BlockSpec((448, 2560), lambda i: (0, i))] * 2,
        out_specs=(pl.BlockSpec((192, 2560), lambda i: (0, i)),) + (whole((448, 192)),) * 4,
        scratch_shapes=[pltpu.VMEM((448, 192), F32)] * 2,
        compiler_params=PARAMS,
        cost_estimate=HINT,
    )(ids, *blocks, own_w, other_w)


def pre_grad_kernel(
    og, out_own, out_other, in_own, in_other, hid_other, slope_own, slope_other,
    row_part, pre_own, send, out_w, in_w, og_w, slope_w, row_w, out_sem, in_sem, og_sem, slope_sem, row_sem,
):
    copy = pltpu.make_async_copy

    def load(source, to, sem, w, j, width):
        at = pl.ds(j * width, width)
        return copy(source.at[:, at], to.at[w, :, at], sem.at[w, j])

    outs, ins = (out_own, out_other), (in_own, in_other)
    pieces = [copy(og.at[j], og_w.at[j], og_sem.at[j]) for j in range(4)]
    slopes = [copy(ref, slope_w.at[w], slope_sem.at[w]) for w, ref in enumerate((slope_own, slope_other))]
    queue = [[pieces[j]] + [load(outs[w], out_w, out_sem, w, j, 896) for w in range(2)] for j in range(4)]
    queue[3] += slopes
    queue += [[load(ins[w], in_w, in_sem, w, j, 1280) for w in range(2)] for j in range(4)]

    def begin(n):
        if n < len(queue):
            for part in queue[n]:
                part.start()

    def arrive(n):
        for part in queue[n]:
            part.wait()
        begin(n + 4)

    for n in range(4):
        begin(n)
    sums = [jnp.zeros((448, 192), F32)] * 2
    for j in range(4):
        arrive(j)
        for w in range(2):
            sums[w] = sums[w] + mm(out_w[w, :, j * 896 : j * 896 + 896], og_w[j], 1, 1)
    own = sums[0] * slope_w[0]
    other = sums[1] * slope_w[1]
    pre_own[...] = own.astype(BF16)
    send[0:448, :] = other.astype(BF16)
    send[448:896, :] = hid_other[...]
    turned = (own.T.astype(BF16), other.T.astype(BF16))
    stores = []
    for j in range(4):
        arrive(4 + j)
        at = slice(j * 1280, j * 1280 + 1280)
        row_w[:, at] = (mm(turned[0], in_w[0, :, at]) + mm(turned[1], in_w[1, :, at])).astype(BF16)
        span = pl.ds(j * 1280, 1280)
        stores.append(copy(row_w.at[:, span], row_part.at[:, span], row_sem.at[j]))
        stores[-1].start()
    for store in stores:
        store.wait()


def pre_grad_of(og, out_own, out_other, in_own, in_other, hid_other, slope_own, slope_other):
    held = pl.BlockSpec(memory_space=pl.ANY)
    return pl.pallas_call(
        pre_grad_kernel,
        out_shape=(struct((192, 5120), BF16), struct((448, 192), BF16), struct((896, 192), BF16)),
        in_specs=[held] * 5 + [VMEM, held, held],
        out_specs=(held, VMEM, VMEM),
        scratch_shapes=[
            pltpu.VMEM((2, 448, 3584), BF16),
            pltpu.VMEM((2, 448, 5120), BF16),
            pltpu.VMEM((4, 192, 896), BF16),
            pltpu.VMEM((2, 448, 192), F32),
            pltpu.VMEM((192, 5120), BF16),
            pltpu.SemaphoreType.DMA((2, 4)),
            pltpu.SemaphoreType.DMA((2, 4)),
            pltpu.SemaphoreType.DMA((4,)),
            pltpu.SemaphoreType.DMA((2,)),
            pltpu.SemaphoreType.DMA((4,)),
        ],
        compiler_params=PARAMS,
        cost_estimate=HINT,
    )(og, out_own, out_other, in_own, in_other, hid_other, slope_own, slope_other)


def x_columns(stk, og, x, out):
    for y in range(4):
        out[:, y * 320 : y * 320 + 320] = stk[:, (4 * y + x) * 320 : (4 * y + x + 1) * 320]
        out[:, 1280 + y * 224 : 1504 + y * 224] = og[y, :, x * 224 : x * 224 + 224]


def weight_grad_kernel(far, ids, stk, stk_other, og, og_other, pre, hid, recv, *outs):
    i = pl.program_id(0)
    turn = 2 if far else jnp.where(i == 2, 3, i)
    x_at, y_at = lax.rem(ids[1] + turn, 4), lax.rem(ids[0] + turn, 4)
    picked, picked_other = outs[-2:]
    for x in range(4):

        @pl.when(x_at == x)
        def _(x=x):
            x_columns(stk, og, x, picked)
            x_columns(stk_other, og_other, x, picked_other)

    across = jnp.concatenate(
        [
            mm(pre[0:224], picked[:, 0:1280]) + mm(recv[0:224], picked_other[:, 0:1280]),
            mm(hid[0:224], picked[:, 1280:2176]) + mm(recv[448:672], picked_other[:, 1280:2176]),
        ],
        axis=1,
    ).astype(BF16)
    at = pl.ds(pl.multiple_of(y_at * 1280, 128), 1280)
    down = jnp.concatenate(
        [
            mm(pre[224:448], stk[:, at]) + mm(recv[224:448], stk_other[:, at]),
            mm(hid[224:448], og[y_at]) + mm(recv[672:896], og_other[y_at]),
        ],
        axis=1,
    ).astype(BF16)
    if far:
        outs[0][...] = across[0:112]
        outs[1][...] = across[112:224]
        outs[2][...] = down[0:112]
        outs[3][...] = down[112:224]
        return
    for k in range(3):

        @pl.when(i == k)
        def _(k=k):
            outs[k][...] = across
            outs[3 + k][...] = down


def weight_grads_of(far, ids, stk, stk_other, og, og_other, pre, hid, recv):
    once = pl.Buffered(buffer_count=1)

    def single(shape):
        return pl.BlockSpec(shape, lambda *_: (0,) * len(shape), pipeline_mode=once)

    def kernel(*refs):
        weight_grad_kernel(far, *refs)

    shapes = [(112, 2176)] * 4 if far else [(224, 2176)] * 6
    return pl.pallas_call(
        kernel,
        out_shape=tuple(struct(shape, BF16) for shape in shapes),
        grid=(1 if far else 3,),
        in_specs=[SMEM]
        + [single((192, 5120))] * 2
        + [single((4, 192, 896))] * 2
        + [single((448, 192)), single((448, 192)), single((896, 192))],
        out_specs=tuple(single(shape) for shape in shapes),
        scratch_shapes=[pltpu.VMEM((192, 2176), BF16)] * 2,
        compiler_params=PARAMS,
        cost_estimate=HINT if far else LONG,
    )(ids, stk, stk_other, og, og_other, pre, hid, recv)


def bump_kernel(x_up, x_down, y_up, y_down, a, b, c, d, *outs):
    for part, got, out in zip((x_up, x_down, y_up, y_down), (a, b, c, d), outs, strict=True):
        out[...] = (part[...].astype(F32) + got[...].astype(F32)).astype(BF16)


def bump_of(x_up, x_down, y_up, y_down, got):
    first = pl.BlockSpec((112, 2176), lambda i: (0, 0))
    second = pl.BlockSpec((112, 2176), lambda i: (1, 0))
    sides = [first, second, first, second]
    return pl.pallas_call(
        bump_kernel,
        out_shape=(struct((224, 2176), BF16),) * 4,
        grid=(1,),
        in_specs=sides + [first] * 4,
        out_specs=tuple(sides),
        input_output_aliases={0: 0, 1: 1, 2: 2, 3: 3},
        compiler_params=PARAMS,
        cost_estimate=HINT,
    )(x_up, x_down, y_up, y_down, *got)


def spread_kernel(where, a, b, c, *outs):
    value = (a[...].astype(F32) + b[...].astype(F32) + c[...].astype(F32)).astype(BF16)
    for n in range(4):
        piece = jnp.concatenate(
            [value[:, n * 320 : n * 320 + 320], value[:, 1280 + n * 224 : 1280 + n * 224 + 224]], axis=1
        )
        turn = lax.rem(n - where[0] + 4, 4)
        for k in range(4):

            @pl.when(turn == k)
            def _(k=k, piece=piece):
                outs[k][...] = piece


def spread_of(where, parts):
    return pl.pallas_call(
        spread_kernel,
        out_shape=(struct((224, 544), BF16),) * 4,
        grid=(2,),
        in_specs=[SMEM] + [pl.BlockSpec((112, 2176), lambda i: (i, 0))] * 3,
        out_specs=(pl.BlockSpec((112, 544), lambda i: (i, 0)),) * 4,
        compiler_params=PARAMS,
        cost_estimate=LONG,
    )(where, *parts)


def finish_kernel(a0, a1, a2, a3, b0, b1, b2, b3, grad_in, grad_out):
    first = a0[...].astype(F32) + a1[...].astype(F32) + a2[...].astype(F32) + a3[...].astype(F32)
    second = b0[...].astype(F32) + b1[...].astype(F32) + b2[...].astype(F32) + b3[...].astype(F32)
    both = jnp.concatenate([first, second], axis=0)
    grad_in[...] = both[:, 0:320].T.astype(BF16)
    grad_out[...] = both[:, 320:544].astype(BF16)


def finish_of(first, second):
    return pl.pallas_call(
        finish_kernel,
        out_shape=(struct((320, 448), BF16), struct((448, 224), BF16)),
        in_specs=[VMEM] * 8,
        out_specs=(VMEM, VMEM),
        compiler_params=PARAMS,
        cost_estimate=LONG,
    )(*first, *second)


def weight_sum_kernel(parts, out):
    total = parts[0].astype(F32)
    for k in range(1, 4):
        total = total + parts[k].astype(F32)
    out[...] = jnp.zeros_like(out)
    for n in range(16):
        out[n, 0:10, :] = total[n * 10 : n * 10 + 10].astype(BF16)


def weight_sum_of(parts):
    return pl.pallas_call(
        weight_sum_kernel,
        out_shape=struct((16, 16, 1280), BF16),
        in_specs=[VMEM],
        out_specs=VMEM,
        compiler_params=SMALL,
        cost_estimate=HINT,
    )(parts)


def ring_of(parts, shift):
    far = lax.ppermute(parts[2], "seq", shift(2))
    up = lax.ppermute(parts[1], "seq", shift(1))
    down = lax.ppermute(parts[3], "seq", shift(-1))
    return (parts[0], up, down, far)


def order_kernel(target, target_other, context, out, out_other):
    for where, to in ((target, out), (target_other, out_other)):
        pick = jnp.where(iota((1280, 128), 0) == where[...], 1.0, 0.0).astype(BF16)
        to[...] = mm(context[...], pick).T.astype(BF16)


def order_of(target, context):
    target = target.reshape(1, 1280)
    return pl.pallas_call(
        order_kernel,
        out_shape=(struct((640, 192), BF16),) * 2,
        grid=(5,),
        in_specs=[
            pl.BlockSpec((1, 128), lambda i: (0, i)),
            pl.BlockSpec((1, 128), lambda i: (0, i + 5)),
            whole((192, 1280)),
        ],
        out_specs=(pl.BlockSpec((128, 192), lambda i: (i, 0)),) * 2,
        compiler_params=SMALL,
        cost_estimate=LONG,
    )(target, target, context)


def out_weight_kernel(ctx, ctx_other, grad, grad_other, out):
    out[...] = (mm(ctx[...], grad[...]) + mm(ctx_other[...], grad_other[...])).astype(BF16)


def out_weight_of(ctx, ctx_other, grad, grad_other):
    block = pl.BlockSpec((192, 256), lambda i: (0, i))
    return pl.pallas_call(
        out_weight_kernel,
        out_shape=struct((640, 1280), BF16),
        grid=(5,),
        in_specs=[whole((640, 192)), whole((640, 192)), block, block],
        out_specs=pl.BlockSpec((640, 256), lambda i: (0, i)),
        compiler_params=SMALL,
        cost_estimate=HINT,
    )(ctx, ctx_other, grad, grad_other)


def swap(value):
    return lax.ppermute(value, "tp", CORE_SWAP)


def z_blocks(block):
    far = lax.ppermute(block, "tp", z_shift(2))
    behind = lax.ppermute(block, "tp", z_shift(1))
    ahead = lax.ppermute(block, "tp", z_shift(-1))
    return (block, ahead, far, behind)


def z_exchange(parts):
    return lax.all_to_all(parts, "tp", split_axis=0, concat_axis=0, axis_index_groups=Z_GROUPS, tiled=True)


def per_device(
    context,
    residual_in,
    out_weight,
    final_norm_weight,
    final_norm_bias,
    adapter_in,
    adapter_out,
    emb_grad,
    group_offsets,
    group_frames,
    group_owner,
):
    s = lax.axis_index("seq")
    t = lax.axis_index("tp")
    c = t % 2
    ids = jnp.stack([s // 4, s % 4, t // 2, c, s]).astype(jnp.int32)
    context = context.reshape(192, 1280)
    residual_in = residual_in.reshape(192, 1280)

    in_own = adapter_in.T
    in_other = swap(in_own)
    out_other = swap(adapter_out)

    parcels = parcels_of(group_offsets, group_frames, group_owner, emb_grad.T)
    arrived = lax.all_to_all(parcels, "seq", split_axis=0, concat_axis=0, tiled=True)
    context, _ = lax.optimization_barrier((context, parcels))
    stacked_here, normed, inverse = encode_of(context, residual_in, out_weight, final_norm_weight, final_norm_bias)
    rows = z_blocks(stacked_here)
    arrived, in_other, out_other, _ = lax.optimization_barrier((arrived, in_other, out_other, stacked_here))

    keep, give = select_of(ids, group_owner, arrived)
    got = swap(give)
    grad_pair = pair_of(ids, keep, got)
    og = z_exchange(grad_pair)

    place = jnp.arange(1280, dtype=jnp.int32)
    core = (place // 640 + c) % 2
    target = (2 * ((place % 640) // 160) + core) * 10 + ((place % 160) // 10) * 80 + place % 10
    context_keep, context_give = order_of(target, context)
    context_got = swap(context_give)

    rows, _ = lax.optimization_barrier((rows, grad_pair))
    stk, hid_own, hid_other, slope_own, slope_other = preact_of(ids, rows, in_own, in_other)
    stk_other = swap(stk)
    og, _ = lax.optimization_barrier((og, context_give))
    og_other = swap(og)
    row_part, pre_own, send = pre_grad_of(
        og, adapter_out, out_other, in_own, in_other, hid_other, slope_own, slope_other
    )
    recv = swap(send)
    row_parts = z_exchange(row_part.reshape(4, 48, 5120))

    pre_own, _ = lax.optimization_barrier((pre_own, row_part))
    operands = (ids, stk, stk_other, og, og_other, pre_own, hid_own, recv)
    x_far, x_far2, y_far, y_far2 = weight_grads_of(True, *operands)
    got = (
        lax.ppermute(x_far, "seq", x_shift(1)),
        lax.ppermute(x_far2, "seq", x_shift(-1)),
        lax.ppermute(y_far, "seq", y_shift(1)),
        lax.ppermute(y_far2, "seq", y_shift(-1)),
    )
    pre_own, _ = lax.optimization_barrier((pre_own, x_far))
    x_here, x_up, x_down, y_here, y_up, y_down = weight_grads_of(
        False, ids, stk, stk_other, og, og_other, pre_own, hid_own, recv
    )
    x_up, x_down, y_up, y_down = bump_of(x_up, x_down, y_up, y_down, got)
    row_parts, _ = lax.optimization_barrier((row_parts, x_up))

    d_residual = norm_back_of(row_parts, normed, inverse, final_norm_weight)
    residual_other = swap(d_residual)
    weight_part = out_weight_of(context_keep, context_got, d_residual, residual_other)
    residual_late, _ = lax.optimization_barrier((d_residual, weight_part))
    d_context = mm(residual_late, out_weight, 1, 1).astype(BF16)
    y_here, _ = lax.optimization_barrier((y_here, d_context))
    y_next = spread_of(
        ids[1:2], (y_here, lax.ppermute(y_up, "seq", y_shift(1)), lax.ppermute(y_down, "seq", y_shift(-1)))
    )
    x_sums = (x_here, lax.ppermute(x_up, "seq", x_shift(1)), lax.ppermute(x_down, "seq", x_shift(-1)))

    weight_parts, _ = lax.optimization_barrier((z_exchange(weight_part.reshape(4, 160, 1280)), y_next[0]))
    weight_z = weight_sum_of(weight_parts)
    pieces = lax.all_to_all(weight_z, "seq", split_axis=0, concat_axis=0, tiled=True)
    d_out_weight = jnp.sum(pieces.astype(F32), axis=0)[:10]

    x_next = spread_of(ids[0:1], x_sums)
    first = ring_of(x_next, y_shift)
    second = ring_of(y_next, x_shift)
    grad_in, grad_out = finish_of(first, second)

    return (
        d_context.reshape(8, 24, 1280),
        d_residual.reshape(8, 24, 1280),
        d_out_weight,
        grad_in,
        grad_out,
    )


def solution(mesh):
    placed = (
        P("seq", "tp", None),
        P("seq", "tp", None),
        P(),
        P(),
        P(),
        P(None, "tp"),
        P("tp", None),
        P("seq", "tp"),
        P(),
        P(),
        P(),
    )
    return jax.shard_map(
        per_device,
        mesh=mesh,
        in_specs=placed,
        out_specs=(
            P("seq", "tp", None),
            P("seq", "tp", None),
            P(("seq", "tp"), None),
            P("seq", "tp"),
            P("tp", "seq"),
        ),
        check_vma=False,
    )
```

```python
import jax
import jax.numpy as jnp
from jax import lax
from jax.experimental import pallas as pl
from jax.experimental.pallas import tpu as pltpu
from jax.sharding import PartitionSpec as P

F32 = jnp.float32
BF16 = jnp.bfloat16
ZN, CN = 4, 2
YN, XN = 4, 4
TP = ZN * CN
PARAMS = pltpu.CompilerParams(vmem_limit_bytes=62 * 1024 * 1024)
SMALL = pltpu.CompilerParams(vmem_limit_bytes=20 * 1024 * 1024)

CORE_SWAP = [(i, i ^ 1) for i in range(TP)]
Z_GROUPS = [[z * CN + c for z in range(ZN)] for c in range(CN)]


def z_shift(step):
    return [(z * CN + c, ((z + step) % ZN) * CN + c) for z in range(ZN) for c in range(CN)]


def x_shift(step):
    return [(y * XN + x, y * XN + (x + step) % XN) for y in range(YN) for x in range(XN)]


def y_shift(step):
    return [(y * XN + x, ((y + step) % YN) * XN + x) for y in range(YN) for x in range(XN)]


def gelu_parts(values):
    cumulative = 0.5 * (1.0 + lax.erf(values * 0.7071067811865476))
    density = jnp.exp(-0.5 * values * values) * 0.3989422804014327
    return values * cumulative, cumulative + values * density


def mm(a, b, ca=1, cb=0):
    return lax.dot_general(a, b, (((ca,), (cb,)), ((), ())), preferred_element_type=F32)


def iota(shape, dim):
    return lax.broadcasted_iota(jnp.int32, shape, dim)


def struct(shape, dtype):
    return jax.ShapeDtypeStruct(shape, dtype)


def whole(shape):
    return pl.BlockSpec(shape, lambda *_: (0,) * len(shape))


SMEM = pl.BlockSpec(memory_space=pltpu.SMEM)
VMEM = pl.BlockSpec(memory_space=pltpu.VMEM)


HINT = pl.CostEstimate(flops=1, bytes_accessed=1, transcendentals=0)
LONG = pl.CostEstimate(flops=40_000_000_000, bytes_accessed=100_000_000, transcendentals=1_000_000)


def parcel_kernel(offsets, frames, owner, grad_t, out):
    out[...] = jnp.zeros_like(out)
    s = lax.axis_index("seq")
    row, col = iota((48, 384), 0), iota((48, 384), 1)
    picks, dests = [], []
    for k in range(8):
        group = s * 8 + k
        start = offsets[group] - s * 384
        count = lax.shift_right_logical(frames[group], 2)
        dests.append(lax.shift_right_logical(owner[group], 3))
        picks.append(jnp.where((row < count) & (col == row + start), 1.0, 0.0))
    tokens = mm(jnp.concatenate(picks).astype(BF16), grad_t[...], 1, 1).astype(BF16)
    for k in range(8):
        out[dests[k]] = tokens[k * 48 : k * 48 + 48]


def parcels_of(offsets, frames, owner, grad_t):
    return pl.pallas_call(
        parcel_kernel,
        out_shape=struct((16, 48, 448), BF16),
        in_specs=[SMEM, SMEM, SMEM, VMEM],
        out_specs=VMEM,
        compiler_params=PARAMS,
        cost_estimate=HINT,
    )(offsets, frames, owner, grad_t)


def select_kernel(ids, owner, arrived, keep, give):
    s, c = ids[4], ids[3]
    row = iota((192, 128), 0)
    z = lax.shift_right_logical(row * 1366, 16)
    rest = row - z * 48
    slot = lax.shift_right_logical(rest * 10923, 16)
    six = rest - slot * 6
    group = iota((192, 128), 1)
    source = jnp.sum(
        jnp.where(owner[...] == s * 8 + slot, lax.shift_right_logical(group, 3), 0), axis=1, keepdims=True
    )
    column = iota((192, 768), 1)
    tokens = arrived[...].reshape(768, 448)
    base = source * 48 + z[:, :1] * 12 + six[:, :1]
    for out, core in ((keep, c), (give, 1 - c)):
        route = jnp.where(column == base + core * 6, 1.0, 0.0).astype(BF16)
        out[...] = mm(route, tokens).astype(BF16)


def select_of(ids, owner, arrived):
    return pl.pallas_call(
        select_kernel,
        out_shape=(struct((192, 448), BF16), struct((192, 448), BF16)),
        in_specs=[SMEM, VMEM, VMEM],
        out_specs=(VMEM, VMEM),
        compiler_params=PARAMS,
        cost_estimate=HINT,
    )(ids, owner.reshape(1, 128), arrived)


def pair_kernel(ids, keep, got, out):
    first = ids[3] == 0
    both = jnp.concatenate(
        [jnp.where(first, keep[...], got[...]), jnp.where(first, got[...], keep[...])], axis=1
    )
    for k in range(4):
        out[k] = both


def pair_of(ids, keep, got):
    return pl.pallas_call(
        pair_kernel,
        out_shape=struct((4, 192, 896), BF16),
        in_specs=[SMEM, VMEM, VMEM],
        out_specs=VMEM,
        compiler_params=PARAMS,
        cost_estimate=HINT,
    )(ids, keep, got)


def encode_kernel(context, residual, weight, gain, bias, stacked, normed, inverse, scratch):
    stream = residual[...].astype(F32) + mm(context[...], weight[...])
    centered = stream - jnp.mean(stream, axis=-1, keepdims=True)
    inv = lax.rsqrt(jnp.mean(centered * centered, axis=-1, keepdims=True) + 1e-05)
    norm = centered * inv
    normed[...] = norm
    inverse[...] = jnp.broadcast_to(inv, inverse.shape)
    encoded = norm * gain[...] + bias[...]
    for piece in range(10):
        scratch[piece] = encoded[:, piece * 128 : (piece + 1) * 128]
    for r in range(4):
        for piece in range(10):
            at = r * 1280 + piece * 128
            stacked[:, at : at + 128] = scratch[piece, pl.ds(r, 48, stride=4), :].astype(BF16)


def encode_of(context, residual, weight, gain, bias):
    return pl.pallas_call(
        encode_kernel,
        out_shape=(struct((48, 5120), BF16), struct((192, 1280), F32), struct((192, 128), F32)),
        in_specs=[VMEM] * 5,
        out_specs=(VMEM,) * 3,
        scratch_shapes=[pltpu.VMEM((10, 192, 128), F32)],
        compiler_params=PARAMS,
        cost_estimate=HINT,
    )(context, residual, weight, gain.reshape(1, 1280), bias.reshape(1, 1280))


def norm_back_kernel(rows, normed, inverse, gain, out, scratch):
    for r in range(4):
        for piece in range(10):
            at = r * 1280 + piece * 128
            total = rows[0, :, at : at + 128].astype(F32)
            for k in range(1, 4):
                total = total + rows[k, :, at : at + 128].astype(F32)
            scratch[piece, pl.ds(r, 48, stride=4), :] = total.astype(BF16).astype(F32)
    scaled = jnp.concatenate([scratch[piece] for piece in range(10)], axis=1) * gain[...]
    norm = normed[...]
    mean = jnp.mean(scaled, axis=-1, keepdims=True)
    along = jnp.mean(scaled * norm, axis=-1, keepdims=True)
    out[...] = (inverse[:, :1] * (scaled - mean - norm * along)).astype(BF16)


def norm_back_of(rows, normed, inverse, gain):
    return pl.pallas_call(
        norm_back_kernel,
        out_shape=struct((192, 1280), BF16),
        in_specs=[VMEM] * 4,
        out_specs=VMEM,
        scratch_shapes=[pltpu.VMEM((10, 192, 128), F32)],
        compiler_params=SMALL,
        cost_estimate=LONG,
    )(rows, normed, inverse, gain.reshape(1, 1280))


def preact_kernel(ids, b0, b1, b2, b3, own_w, other_w, stk, hid_own, hid_other, slope_own, slope_other, acc, acc_other):
    i = pl.program_id(0)
    for step, block in enumerate((b0, b1, b2, b3)):
        at = pl.multiple_of(lax.rem(ids[2] + step, 4) * 48, 16)
        stk[pl.ds(at, 48), :] = block[...]

    @pl.when(i == 0)
    def _():
        acc[...] = jnp.zeros_like(acc)
        acc_other[...] = jnp.zeros_like(acc_other)

    rows = stk[...]
    acc[...] += mm(own_w[...], rows, 1, 1)
    acc_other[...] += mm(other_w[...], rows, 1, 1)

    @pl.when(i == pl.num_programs(0) - 1)
    def _():
        hidden, slope = gelu_parts(acc[...])
        hid_own[...] = hidden.astype(BF16)
        slope_own[...] = slope
        hidden, slope = gelu_parts(acc_other[...])
        hid_other[...] = hidden.astype(BF16)
        slope_other[...] = slope


def preact_of(ids, blocks, own_w, other_w):
    return pl.pallas_call(
        preact_kernel,
        out_shape=(
            struct((192, 5120), BF16),
            struct((448, 192), BF16),
            struct((448, 192), BF16),
            struct((448, 192), F32),
            struct((448, 192), F32),
        ),
        grid=(2,),
        in_specs=[SMEM]
        + [pl.BlockSpec((48, 2560), lambda i: (0, i))] * 4
        + [pl.BlockSpec((448, 2560), lambda i: (0, i))] * 2,
        out_specs=(pl.BlockSpec((192, 2560), lambda i: (0, i)),) + (whole((448, 192)),) * 4,
        scratch_shapes=[pltpu.VMEM((448, 192), F32)] * 2,
        compiler_params=PARAMS,
        cost_estimate=HINT,
    )(ids, *blocks, own_w, other_w)


def pre_grad_kernel(
    og, out_own, out_other, in_own, in_other, hid_other, slope_own, slope_other,
    row_part, pre_own, send, out_w, in_w, og_w, slope_w, row_w, out_sem, in_sem, og_sem, slope_sem, row_sem,
):
    copy = pltpu.make_async_copy

    def load(source, to, sem, w, j, width):
        at = pl.ds(j * width, width)
        return copy(source.at[:, at], to.at[w, :, at], sem.at[w, j])

    outs, ins = (out_own, out_other), (in_own, in_other)
    pieces = [copy(og.at[j], og_w.at[j], og_sem.at[j]) for j in range(4)]
    slopes = [copy(ref, slope_w.at[w], slope_sem.at[w]) for w, ref in enumerate((slope_own, slope_other))]
    queue = [[pieces[j]] + [load(outs[w], out_w, out_sem, w, j, 896) for w in range(2)] for j in range(4)]
    queue[3] += slopes
    queue += [[load(ins[w], in_w, in_sem, w, j, 1280) for w in range(2)] for j in range(4)]

    def begin(n):
        if n < len(queue):
            for part in queue[n]:
                part.start()

    def arrive(n):
        for part in queue[n]:
            part.wait()
        begin(n + 4)

    for n in range(4):
        begin(n)
    sums = [jnp.zeros((448, 192), F32)] * 2
    for j in range(4):
        arrive(j)
        for w in range(2):
            sums[w] = sums[w] + mm(out_w[w, :, j * 896 : j * 896 + 896], og_w[j], 1, 1)
    own = sums[0] * slope_w[0]
    other = sums[1] * slope_w[1]
    pre_own[...] = own.astype(BF16)
    send[0:448, :] = other.astype(BF16)
    send[448:896, :] = hid_other[...]
    turned = (own.T.astype(BF16), other.T.astype(BF16))
    stores = []
    for j in range(4):
        arrive(4 + j)
        at = slice(j * 1280, j * 1280 + 1280)
        row_w[:, at] = (mm(turned[0], in_w[0, :, at]) + mm(turned[1], in_w[1, :, at])).astype(BF16)
        span = pl.ds(j * 1280, 1280)
        stores.append(copy(row_w.at[:, span], row_part.at[:, span], row_sem.at[j]))
        stores[-1].start()
    for store in stores:
        store.wait()


def pre_grad_of(og, out_own, out_other, in_own, in_other, hid_other, slope_own, slope_other):
    held = pl.BlockSpec(memory_space=pl.ANY)
    return pl.pallas_call(
        pre_grad_kernel,
        out_shape=(struct((192, 5120), BF16), struct((448, 192), BF16), struct((896, 192), BF16)),
        in_specs=[held] * 5 + [VMEM, held, held],
        out_specs=(held, VMEM, VMEM),
        scratch_shapes=[
            pltpu.VMEM((2, 448, 3584), BF16),
            pltpu.VMEM((2, 448, 5120), BF16),
            pltpu.VMEM((4, 192, 896), BF16),
            pltpu.VMEM((2, 448, 192), F32),
            pltpu.VMEM((192, 5120), BF16),
            pltpu.SemaphoreType.DMA((2, 4)),
            pltpu.SemaphoreType.DMA((2, 4)),
            pltpu.SemaphoreType.DMA((4,)),
            pltpu.SemaphoreType.DMA((2,)),
            pltpu.SemaphoreType.DMA((4,)),
        ],
        compiler_params=PARAMS,
        cost_estimate=HINT,
    )(og, out_own, out_other, in_own, in_other, hid_other, slope_own, slope_other)


def x_columns(stk, og, x, out):
    for y in range(4):
        out[:, y * 320 : y * 320 + 320] = stk[:, (4 * y + x) * 320 : (4 * y + x + 1) * 320]
        out[:, 1280 + y * 224 : 1504 + y * 224] = og[y, :, x * 224 : x * 224 + 224]


def weight_grad_kernel(far, ids, stk, stk_other, og, og_other, pre, hid, recv, *outs):
    i = pl.program_id(0)
    turn = 2 if far else jnp.where(i == 2, 3, i)
    x_at, y_at = lax.rem(ids[1] + turn, 4), lax.rem(ids[0] + turn, 4)
    picked, picked_other = outs[-2:]
    for x in range(4):

        @pl.when(x_at == x)
        def _(x=x):
            x_columns(stk, og, x, picked)
            x_columns(stk_other, og_other, x, picked_other)

    across = jnp.concatenate(
        [
            mm(pre[0:224], picked[:, 0:1280]) + mm(recv[0:224], picked_other[:, 0:1280]),
            mm(hid[0:224], picked[:, 1280:2176]) + mm(recv[448:672], picked_other[:, 1280:2176]),
        ],
        axis=1,
    ).astype(BF16)
    at = pl.ds(pl.multiple_of(y_at * 1280, 128), 1280)
    down = jnp.concatenate(
        [
            mm(pre[224:448], stk[:, at]) + mm(recv[224:448], stk_other[:, at]),
            mm(hid[224:448], og[y_at]) + mm(recv[672:896], og_other[y_at]),
        ],
        axis=1,
    ).astype(BF16)
    if far:
        outs[0][...] = across[0:112]
        outs[1][...] = across[112:224]
        outs[2][...] = down[0:112]
        outs[3][...] = down[112:224]
        return
    for k in range(3):

        @pl.when(i == k)
        def _(k=k):
            outs[k][...] = across
            outs[3 + k][...] = down


def weight_grads_of(far, ids, stk, stk_other, og, og_other, pre, hid, recv):
    once = pl.Buffered(buffer_count=1)

    def single(shape):
        return pl.BlockSpec(shape, lambda *_: (0,) * len(shape), pipeline_mode=once)

    def kernel(*refs):
        weight_grad_kernel(far, *refs)

    shapes = [(112, 2176)] * 4 if far else [(224, 2176)] * 6
    return pl.pallas_call(
        kernel,
        out_shape=tuple(struct(shape, BF16) for shape in shapes),
        grid=(1 if far else 3,),
        in_specs=[SMEM]
        + [single((192, 5120))] * 2
        + [single((4, 192, 896))] * 2
        + [single((448, 192)), single((448, 192)), single((896, 192))],
        out_specs=tuple(single(shape) for shape in shapes),
        scratch_shapes=[pltpu.VMEM((192, 2176), BF16)] * 2,
        compiler_params=PARAMS,
        cost_estimate=HINT if far else LONG,
    )(ids, stk, stk_other, og, og_other, pre, hid, recv)


def bump_kernel(x_up, x_down, y_up, y_down, a, b, c, d, *outs):
    for part, got, out in zip((x_up, x_down, y_up, y_down), (a, b, c, d), outs, strict=True):
        out[...] = (part[...].astype(F32) + got[...].astype(F32)).astype(BF16)


def bump_of(x_up, x_down, y_up, y_down, got):
    first = pl.BlockSpec((112, 2176), lambda i: (0, 0))
    second = pl.BlockSpec((112, 2176), lambda i: (1, 0))
    sides = [first, second, first, second]
    return pl.pallas_call(
        bump_kernel,
        out_shape=(struct((224, 2176), BF16),) * 4,
        grid=(1,),
        in_specs=sides + [first] * 4,
        out_specs=tuple(sides),
        input_output_aliases={0: 0, 1: 1, 2: 2, 3: 3},
        compiler_params=PARAMS,
        cost_estimate=HINT,
    )(x_up, x_down, y_up, y_down, *got)


def spread_kernel(where, a, b, c, *outs):
    value = (a[...].astype(F32) + b[...].astype(F32) + c[...].astype(F32)).astype(BF16)
    for n in range(4):
        piece = jnp.concatenate(
            [value[:, n * 320 : n * 320 + 320], value[:, 1280 + n * 224 : 1280 + n * 224 + 224]], axis=1
        )
        turn = lax.rem(n - where[0] + 4, 4)
        for k in range(4):

            @pl.when(turn == k)
            def _(k=k, piece=piece):
                outs[k][...] = piece


def spread_of(where, parts):
    return pl.pallas_call(
        spread_kernel,
        out_shape=(struct((224, 544), BF16),) * 4,
        grid=(2,),
        in_specs=[SMEM] + [pl.BlockSpec((112, 2176), lambda i: (i, 0))] * 3,
        out_specs=(pl.BlockSpec((112, 544), lambda i: (i, 0)),) * 4,
        compiler_params=PARAMS,
        cost_estimate=LONG,
    )(where, *parts)


def finish_kernel(a0, a1, a2, a3, b0, b1, b2, b3, grad_in, grad_out):
    first = a0[...].astype(F32) + a1[...].astype(F32) + a2[...].astype(F32) + a3[...].astype(F32)
    second = b0[...].astype(F32) + b1[...].astype(F32) + b2[...].astype(F32) + b3[...].astype(F32)
    both = jnp.concatenate([first, second], axis=0)
    grad_in[...] = both[:, 0:320].T.astype(BF16)
    grad_out[...] = both[:, 320:544].astype(BF16)


def finish_of(first, second):
    return pl.pallas_call(
        finish_kernel,
        out_shape=(struct((320, 448), BF16), struct((448, 224), BF16)),
        in_specs=[VMEM] * 8,
        out_specs=(VMEM, VMEM),
        compiler_params=PARAMS,
        cost_estimate=LONG,
    )(*first, *second)


def weight_sum_kernel(parts, out):
    total = parts[0].astype(F32)
    for k in range(1, 4):
        total = total + parts[k].astype(F32)
    out[...] = jnp.zeros_like(out)
    for n in range(16):
        out[n, 0:10, :] = total[n * 10 : n * 10 + 10].astype(BF16)


def weight_sum_of(parts):
    return pl.pallas_call(
        weight_sum_kernel,
        out_shape=struct((16, 16, 1280), BF16),
        in_specs=[VMEM],
        out_specs=VMEM,
        compiler_params=SMALL,
        cost_estimate=HINT,
    )(parts)


def ring_of(parts, shift):
    far = lax.ppermute(parts[2], "seq", shift(2))
    up = lax.ppermute(parts[1], "seq", shift(1))
    down = lax.ppermute(parts[3], "seq", shift(-1))
    return (parts[0], up, down, far)


def order_kernel(target, target_other, context, out, out_other):
    for where, to in ((target, out), (target_other, out_other)):
        pick = jnp.where(iota((1280, 128), 0) == where[...], 1.0, 0.0).astype(BF16)
        to[...] = mm(context[...], pick).T.astype(BF16)


def order_of(target, context):
    target = target.reshape(1, 1280)
    return pl.pallas_call(
        order_kernel,
        out_shape=(struct((640, 192), BF16),) * 2,
        grid=(5,),
        in_specs=[
            pl.BlockSpec((1, 128), lambda i: (0, i)),
            pl.BlockSpec((1, 128), lambda i: (0, i + 5)),
            whole((192, 1280)),
        ],
        out_specs=(pl.BlockSpec((128, 192), lambda i: (i, 0)),) * 2,
        compiler_params=SMALL,
        cost_estimate=LONG,
    )(target, target, context)


def out_weight_kernel(ctx, ctx_other, grad, grad_other, out):
    out[...] = (mm(ctx[...], grad[...]) + mm(ctx_other[...], grad_other[...])).astype(BF16)


def out_weight_of(ctx, ctx_other, grad, grad_other):
    block = pl.BlockSpec((192, 256), lambda i: (0, i))
    return pl.pallas_call(
        out_weight_kernel,
        out_shape=struct((640, 1280), BF16),
        grid=(5,),
        in_specs=[whole((640, 192)), whole((640, 192)), block, block],
        out_specs=pl.BlockSpec((640, 256), lambda i: (0, i)),
        compiler_params=SMALL,
        cost_estimate=HINT,
    )(ctx, ctx_other, grad, grad_other)


def swap(value):
    return lax.ppermute(value, "tp", CORE_SWAP)


def z_blocks(block):
    far = lax.ppermute(block, "tp", z_shift(2))
    behind = lax.ppermute(block, "tp", z_shift(1))
    ahead = lax.ppermute(block, "tp", z_shift(-1))
    return (block, ahead, far, behind)


def z_exchange(parts):
    return lax.all_to_all(parts, "tp", split_axis=0, concat_axis=0, axis_index_groups=Z_GROUPS, tiled=True)


def per_device(
    context,
    residual_in,
    out_weight,
    final_norm_weight,
    final_norm_bias,
    adapter_in,
    adapter_out,
    emb_grad,
    group_offsets,
    group_frames,
    group_owner,
):
    s = lax.axis_index("seq")
    t = lax.axis_index("tp")
    c = t % 2
    ids = jnp.stack([s // 4, s % 4, t // 2, c, s]).astype(jnp.int32)
    context = context.reshape(192, 1280)
    residual_in = residual_in.reshape(192, 1280)

    in_own = adapter_in.T
    in_other = swap(in_own)
    out_other = swap(adapter_out)

    parcels = parcels_of(group_offsets, group_frames, group_owner, emb_grad.T)
    arrived = lax.all_to_all(parcels, "seq", split_axis=0, concat_axis=0, tiled=True)
    context, _ = lax.optimization_barrier((context, parcels))
    stacked_here, normed, inverse = encode_of(context, residual_in, out_weight, final_norm_weight, final_norm_bias)
    rows = z_blocks(stacked_here)
    arrived, in_other, out_other, _ = lax.optimization_barrier((arrived, in_other, out_other, stacked_here))

    keep, give = select_of(ids, group_owner, arrived)
    got = swap(give)
    grad_pair = pair_of(ids, keep, got)
    og = z_exchange(grad_pair)

    place = jnp.arange(1280, dtype=jnp.int32)
    core = (place // 640 + c) % 2
    target = (2 * ((place % 640) // 160) + core) * 10 + ((place % 160) // 10) * 80 + place % 10
    context_keep, context_give = order_of(target, context)
    context_got = swap(context_give)

    rows, _ = lax.optimization_barrier((rows, grad_pair))
    stk, hid_own, hid_other, slope_own, slope_other = preact_of(ids, rows, in_own, in_other)
    stk_other = swap(stk)
    og, _ = lax.optimization_barrier((og, context_give))
    og_other = swap(og)
    row_part, pre_own, send = pre_grad_of(
        og, adapter_out, out_other, in_own, in_other, hid_other, slope_own, slope_other
    )
    recv = swap(send)
    row_parts = z_exchange(row_part.reshape(4, 48, 5120))

    pre_own, _ = lax.optimization_barrier((pre_own, row_part))
    operands = (ids, stk, stk_other, og, og_other, pre_own, hid_own, recv)
    x_far, x_far2, y_far, y_far2 = weight_grads_of(True, *operands)
    got = (
        lax.ppermute(x_far, "seq", x_shift(1)),
        lax.ppermute(x_far2, "seq", x_shift(-1)),
        lax.ppermute(y_far, "seq", y_shift(1)),
        lax.ppermute(y_far2, "seq", y_shift(-1)),
    )
    pre_own, _ = lax.optimization_barrier((pre_own, x_far))
    x_here, x_up, x_down, y_here, y_up, y_down = weight_grads_of(
        False, ids, stk, stk_other, og, og_other, pre_own, hid_own, recv
    )
    x_up, x_down, y_up, y_down = bump_of(x_up, x_down, y_up, y_down, got)
    row_parts, _ = lax.optimization_barrier((row_parts, x_up))

    d_residual = norm_back_of(row_parts, normed, inverse, final_norm_weight)
    residual_other = swap(d_residual)
    weight_part = out_weight_of(context_keep, context_got, d_residual, residual_other)
    residual_late, _ = lax.optimization_barrier((d_residual, weight_part))
    d_context = mm(residual_late, out_weight, 1, 1).astype(BF16)
    y_here, _ = lax.optimization_barrier((y_here, d_context))
    y_next = spread_of(
        ids[1:2], (y_here, lax.ppermute(y_up, "seq", y_shift(1)), lax.ppermute(y_down, "seq", y_shift(-1)))
    )
    x_sums = (x_here, lax.ppermute(x_up, "seq", x_shift(1)), lax.ppermute(x_down, "seq", x_shift(-1)))

    weight_parts, _ = lax.optimization_barrier((z_exchange(weight_part.reshape(4, 160, 1280)), y_next[0]))
    weight_z = weight_sum_of(weight_parts)
    pieces = lax.all_to_all(weight_z, "seq", split_axis=0, concat_axis=0, tiled=True)
    d_out_weight = jnp.sum(pieces.astype(F32), axis=0)[:10]

    x_next = spread_of(ids[0:1], x_sums)
    first = ring_of(x_next, y_shift)
    second = ring_of(y_next, x_shift)
    grad_in, grad_out = finish_of(first, second)

    return (
        d_context.reshape(8, 24, 1280),
        d_residual.reshape(8, 24, 1280),
        d_out_weight,
        grad_in,
        grad_out,
    )


def solution(mesh):
    placed = (
        P("seq", "tp", None),
        P("seq", "tp", None),
        P(),
        P(),
        P(),
        P(None, "tp"),
        P("tp", None),
        P("seq", "tp"),
        P(),
        P(),
        P(),
    )
    return jax.shard_map(
        per_device,
        mesh=mesh,
        in_specs=placed,
        out_specs=(
            P("seq", "tp", None),
            P("seq", "tp", None),
            P(("seq", "tp"), None),
            P("seq", "tp"),
            P("tp", "seq"),
        ),
        check_vma=False,
    )
```

```python
import jax
import jax.numpy as jnp
from jax import lax
from jax.experimental import pallas as pl
from jax.experimental.pallas import tpu as pltpu
from jax.sharding import PartitionSpec as P

F32 = jnp.float32
BF16 = jnp.bfloat16
ZN, CN = 4, 2
YN, XN = 4, 4
TP = ZN * CN
PARAMS = pltpu.CompilerParams(vmem_limit_bytes=62 * 1024 * 1024)
SMALL = pltpu.CompilerParams(vmem_limit_bytes=20 * 1024 * 1024)

CORE_SWAP = [(i, i ^ 1) for i in range(TP)]
Z_GROUPS = [[z * CN + c for z in range(ZN)] for c in range(CN)]


def z_shift(step):
    return [(z * CN + c, ((z + step) % ZN) * CN + c) for z in range(ZN) for c in range(CN)]


def x_shift(step):
    return [(y * XN + x, y * XN + (x + step) % XN) for y in range(YN) for x in range(XN)]


def y_shift(step):
    return [(y * XN + x, ((y + step) % YN) * XN + x) for y in range(YN) for x in range(XN)]


def gelu_parts(values):
    cumulative = 0.5 * (1.0 + lax.erf(values * 0.7071067811865476))
    density = jnp.exp(-0.5 * values * values) * 0.3989422804014327
    return values * cumulative, cumulative + values * density


def mm(a, b, ca=1, cb=0):
    return lax.dot_general(a, b, (((ca,), (cb,)), ((), ())), preferred_element_type=F32)


def iota(shape, dim):
    return lax.broadcasted_iota(jnp.int32, shape, dim)


def struct(shape, dtype):
    return jax.ShapeDtypeStruct(shape, dtype)


def whole(shape):
    return pl.BlockSpec(shape, lambda *_: (0,) * len(shape))


SMEM = pl.BlockSpec(memory_space=pltpu.SMEM)
VMEM = pl.BlockSpec(memory_space=pltpu.VMEM)


HINT = pl.CostEstimate(flops=1, bytes_accessed=1, transcendentals=0)
LONG = pl.CostEstimate(flops=40_000_000_000, bytes_accessed=100_000_000, transcendentals=1_000_000)


def parcel_kernel(offsets, frames, owner, grad_t, out):
    out[...] = jnp.zeros_like(out)
    s = lax.axis_index("seq")
    row, col = iota((48, 384), 0), iota((48, 384), 1)
    picks, dests = [], []
    for k in range(8):
        group = s * 8 + k
        start = offsets[group] - s * 384
        count = lax.shift_right_logical(frames[group], 2)
        dests.append(lax.shift_right_logical(owner[group], 3))
        picks.append(jnp.where((row < count) & (col == row + start), 1.0, 0.0))
    tokens = mm(jnp.concatenate(picks).astype(BF16), grad_t[...], 1, 1).astype(BF16)
    for k in range(8):
        out[dests[k]] = tokens[k * 48 : k * 48 + 48]


def parcels_of(offsets, frames, owner, grad_t):
    return pl.pallas_call(
        parcel_kernel,
        out_shape=struct((16, 48, 448), BF16),
        in_specs=[SMEM, SMEM, SMEM, VMEM],
        out_specs=VMEM,
        compiler_params=PARAMS,
        cost_estimate=HINT,
    )(offsets, frames, owner, grad_t)


def select_kernel(ids, owner, arrived, keep, give):
    s, c = ids[4], ids[3]
    row = iota((192, 128), 0)
    z = lax.shift_right_logical(row * 1366, 16)
    rest = row - z * 48
    slot = lax.shift_right_logical(rest * 10923, 16)
    six = rest - slot * 6
    group = iota((192, 128), 1)
    source = jnp.sum(
        jnp.where(owner[...] == s * 8 + slot, lax.shift_right_logical(group, 3), 0), axis=1, keepdims=True
    )
    column = iota((192, 768), 1)
    tokens = arrived[...].reshape(768, 448)
    base = source * 48 + z[:, :1] * 12 + six[:, :1]
    for out, core in ((keep, c), (give, 1 - c)):
        route = jnp.where(column == base + core * 6, 1.0, 0.0).astype(BF16)
        out[...] = mm(route, tokens).astype(BF16)


def select_of(ids, owner, arrived):
    return pl.pallas_call(
        select_kernel,
        out_shape=(struct((192, 448), BF16), struct((192, 448), BF16)),
        in_specs=[SMEM, VMEM, VMEM],
        out_specs=(VMEM, VMEM),
        compiler_params=PARAMS,
        cost_estimate=HINT,
    )(ids, owner.reshape(1, 128), arrived)


def pair_kernel(ids, keep, got, out):
    first = ids[3] == 0
    both = jnp.concatenate(
        [jnp.where(first, keep[...], got[...]), jnp.where(first, got[...], keep[...])], axis=1
    )
    for k in range(4):
        out[k] = both


def pair_of(ids, keep, got):
    return pl.pallas_call(
        pair_kernel,
        out_shape=struct((4, 192, 896), BF16),
        in_specs=[SMEM, VMEM, VMEM],
        out_specs=VMEM,
        compiler_params=PARAMS,
        cost_estimate=HINT,
    )(ids, keep, got)


def encode_kernel(context, residual, weight, gain, bias, stacked, normed, inverse, scratch):
    stream = residual[...].astype(F32) + mm(context[...], weight[...])
    centered = stream - jnp.mean(stream, axis=-1, keepdims=True)
    inv = lax.rsqrt(jnp.mean(centered * centered, axis=-1, keepdims=True) + 1e-05)
    norm = centered * inv
    normed[...] = norm
    inverse[...] = jnp.broadcast_to(inv, inverse.shape)
    encoded = norm * gain[...] + bias[...]
    for piece in range(10):
        scratch[piece] = encoded[:, piece * 128 : (piece + 1) * 128]
    for r in range(4):
        for piece in range(10):
            at = r * 1280 + piece * 128
            stacked[:, at : at + 128] = scratch[piece, pl.ds(r, 48, stride=4), :].astype(BF16)


def encode_of(context, residual, weight, gain, bias):
    return pl.pallas_call(
        encode_kernel,
        out_shape=(struct((48, 5120), BF16), struct((192, 1280), F32), struct((192, 128), F32)),
        in_specs=[VMEM] * 5,
        out_specs=(VMEM,) * 3,
        scratch_shapes=[pltpu.VMEM((10, 192, 128), F32)],
        compiler_params=PARAMS,
        cost_estimate=HINT,
    )(context, residual, weight, gain.reshape(1, 1280), bias.reshape(1, 1280))


def norm_back_kernel(rows, normed, inverse, gain, out, scratch):
    for r in range(4):
        for piece in range(10):
            at = r * 1280 + piece * 128
            total = rows[0, :, at : at + 128].astype(F32)
            for k in range(1, 4):
                total = total + rows[k, :, at : at + 128].astype(F32)
            scratch[piece, pl.ds(r, 48, stride=4), :] = total.astype(BF16).astype(F32)
    scaled = jnp.concatenate([scratch[piece] for piece in range(10)], axis=1) * gain[...]
    norm = normed[...]
    mean = jnp.mean(scaled, axis=-1, keepdims=True)
    along = jnp.mean(scaled * norm, axis=-1, keepdims=True)
    out[...] = (inverse[:, :1] * (scaled - mean - norm * along)).astype(BF16)


def norm_back_of(rows, normed, inverse, gain):
    return pl.pallas_call(
        norm_back_kernel,
        out_shape=struct((192, 1280), BF16),
        in_specs=[VMEM] * 4,
        out_specs=VMEM,
        scratch_shapes=[pltpu.VMEM((10, 192, 128), F32)],
        compiler_params=SMALL,
        cost_estimate=LONG,
    )(rows, normed, inverse, gain.reshape(1, 1280))


def preact_kernel(ids, b0, b1, b2, b3, own_w, other_w, stk, hid_own, hid_other, slope_own, slope_other, acc, acc_other):
    i = pl.program_id(0)
    for step, block in enumerate((b0, b1, b2, b3)):
        at = pl.multiple_of(lax.rem(ids[2] + step, 4) * 48, 16)
        stk[pl.ds(at, 48), :] = block[...]

    @pl.when(i == 0)
    def _():
        acc[...] = jnp.zeros_like(acc)
        acc_other[...] = jnp.zeros_like(acc_other)

    rows = stk[...]
    acc[...] += mm(own_w[...], rows, 1, 1)
    acc_other[...] += mm(other_w[...], rows, 1, 1)

    @pl.when(i == pl.num_programs(0) - 1)
    def _():
        hidden, slope = gelu_parts(acc[...])
        hid_own[...] = hidden.astype(BF16)
        slope_own[...] = slope
        hidden, slope = gelu_parts(acc_other[...])
        hid_other[...] = hidden.astype(BF16)
        slope_other[...] = slope


def preact_of(ids, blocks, own_w, other_w):
    return pl.pallas_call(
        preact_kernel,
        out_shape=(
            struct((192, 5120), BF16),
            struct((448, 192), BF16),
            struct((448, 192), BF16),
            struct((448, 192), F32),
            struct((448, 192), F32),
        ),
        grid=(2,),
        in_specs=[SMEM]
        + [pl.BlockSpec((48, 2560), lambda i: (0, i))] * 4
        + [pl.BlockSpec((448, 2560), lambda i: (0, i))] * 2,
        out_specs=(pl.BlockSpec((192, 2560), lambda i: (0, i)),) + (whole((448, 192)),) * 4,
        scratch_shapes=[pltpu.VMEM((448, 192), F32)] * 2,
        compiler_params=PARAMS,
        cost_estimate=HINT,
    )(ids, *blocks, own_w, other_w)


def pre_grad_kernel(
    og, out_own, out_other, in_own, in_other, hid_other, slope_own, slope_other,
    row_part, pre_own, send, out_w, in_w, og_w, slope_w, row_w, out_sem, in_sem, og_sem, slope_sem, row_sem,
):
    copy = pltpu.make_async_copy

    def load(source, to, sem, w, j, width):
        at = pl.ds(j * width, width)
        return copy(source.at[:, at], to.at[w, :, at], sem.at[w, j])

    outs, ins = (out_own, out_other), (in_own, in_other)
    pieces = [copy(og.at[j], og_w.at[j], og_sem.at[j]) for j in range(4)]
    slopes = [copy(ref, slope_w.at[w], slope_sem.at[w]) for w, ref in enumerate((slope_own, slope_other))]
    queue = [[pieces[j]] + [load(outs[w], out_w, out_sem, w, j, 896) for w in range(2)] for j in range(4)]
    queue[3] += slopes
    queue += [[load(ins[w], in_w, in_sem, w, j, 1280) for w in range(2)] for j in range(4)]

    def begin(n):
        if n < len(queue):
            for part in queue[n]:
                part.start()

    def arrive(n):
        for part in queue[n]:
            part.wait()
        begin(n + 4)

    for n in range(4):
        begin(n)
    sums = [jnp.zeros((448, 192), F32)] * 2
    for j in range(4):
        arrive(j)
        for w in range(2):
            sums[w] = sums[w] + mm(out_w[w, :, j * 896 : j * 896 + 896], og_w[j], 1, 1)
    own = sums[0] * slope_w[0]
    other = sums[1] * slope_w[1]
    pre_own[...] = own.astype(BF16)
    send[0:448, :] = other.astype(BF16)
    send[448:896, :] = hid_other[...]
    turned = (own.T.astype(BF16), other.T.astype(BF16))
    stores = []
    for j in range(4):
        arrive(4 + j)
        at = slice(j * 1280, j * 1280 + 1280)
        row_w[:, at] = (mm(turned[0], in_w[0, :, at]) + mm(turned[1], in_w[1, :, at])).astype(BF16)
        span = pl.ds(j * 1280, 1280)
        stores.append(copy(row_w.at[:, span], row_part.at[:, span], row_sem.at[j]))
        stores[-1].start()
    for store in stores:
        store.wait()


def pre_grad_of(og, out_own, out_other, in_own, in_other, hid_other, slope_own, slope_other):
    held = pl.BlockSpec(memory_space=pl.ANY)
    return pl.pallas_call(
        pre_grad_kernel,
        out_shape=(struct((192, 5120), BF16), struct((448, 192), BF16), struct((896, 192), BF16)),
        in_specs=[held] * 5 + [VMEM, held, held],
        out_specs=(held, VMEM, VMEM),
        scratch_shapes=[
            pltpu.VMEM((2, 448, 3584), BF16),
            pltpu.VMEM((2, 448, 5120), BF16),
            pltpu.VMEM((4, 192, 896), BF16),
            pltpu.VMEM((2, 448, 192), F32),
            pltpu.VMEM((192, 5120), BF16),
            pltpu.SemaphoreType.DMA((2, 4)),
            pltpu.SemaphoreType.DMA((2, 4)),
            pltpu.SemaphoreType.DMA((4,)),
            pltpu.SemaphoreType.DMA((2,)),
            pltpu.SemaphoreType.DMA((4,)),
        ],
        compiler_params=PARAMS,
        cost_estimate=HINT,
    )(og, out_own, out_other, in_own, in_other, hid_other, slope_own, slope_other)


def x_columns(stk, og, x, out):
    for y in range(4):
        out[:, y * 320 : y * 320 + 320] = stk[:, (4 * y + x) * 320 : (4 * y + x + 1) * 320]
        out[:, 1280 + y * 224 : 1504 + y * 224] = og[y, :, x * 224 : x * 224 + 224]


def weight_grad_kernel(far, ids, stk, stk_other, og, og_other, pre, hid, recv, *outs):
    i = pl.program_id(0)
    turn = 2 if far else jnp.where(i == 2, 3, i)
    x_at, y_at = lax.rem(ids[1] + turn, 4), lax.rem(ids[0] + turn, 4)
    picked, picked_other = outs[-2:]
    for x in range(4):

        @pl.when(x_at == x)
        def _(x=x):
            x_columns(stk, og, x, picked)
            x_columns(stk_other, og_other, x, picked_other)

    across = jnp.concatenate(
        [
            mm(pre[0:224], picked[:, 0:1280]) + mm(recv[0:224], picked_other[:, 0:1280]),
            mm(hid[0:224], picked[:, 1280:2176]) + mm(recv[448:672], picked_other[:, 1280:2176]),
        ],
        axis=1,
    ).astype(BF16)
    at = pl.ds(pl.multiple_of(y_at * 1280, 128), 1280)
    down = jnp.concatenate(
        [
            mm(pre[224:448], stk[:, at]) + mm(recv[224:448], stk_other[:, at]),
            mm(hid[224:448], og[y_at]) + mm(recv[672:896], og_other[y_at]),
        ],
        axis=1,
    ).astype(BF16)
    if far:
        outs[0][...] = across[0:112]
        outs[1][...] = across[112:224]
        outs[2][...] = down[0:112]
        outs[3][...] = down[112:224]
        return
    for k in range(3):

        @pl.when(i == k)
        def _(k=k):
            outs[k][...] = across
            outs[3 + k][...] = down


def weight_grads_of(far, ids, stk, stk_other, og, og_other, pre, hid, recv):
    once = pl.Buffered(buffer_count=1)

    def single(shape):
        return pl.BlockSpec(shape, lambda *_: (0,) * len(shape), pipeline_mode=once)

    def kernel(*refs):
        weight_grad_kernel(far, *refs)

    shapes = [(112, 2176)] * 4 if far else [(224, 2176)] * 6
    return pl.pallas_call(
        kernel,
        out_shape=tuple(struct(shape, BF16) for shape in shapes),
        grid=(1 if far else 3,),
        in_specs=[SMEM]
        + [single((192, 5120))] * 2
        + [single((4, 192, 896))] * 2
        + [single((448, 192)), single((448, 192)), single((896, 192))],
        out_specs=tuple(single(shape) for shape in shapes),
        scratch_shapes=[pltpu.VMEM((192, 2176), BF16)] * 2,
        compiler_params=PARAMS,
        cost_estimate=HINT if far else LONG,
    )(ids, stk, stk_other, og, og_other, pre, hid, recv)


def bump_kernel(x_up, x_down, y_up, y_down, a, b, c, d, *outs):
    for part, got, out in zip((x_up, x_down, y_up, y_down), (a, b, c, d), outs, strict=True):
        out[...] = (part[...].astype(F32) + got[...].astype(F32)).astype(BF16)


def bump_of(x_up, x_down, y_up, y_down, got):
    first = pl.BlockSpec((112, 2176), lambda i: (0, 0))
    second = pl.BlockSpec((112, 2176), lambda i: (1, 0))
    sides = [first, second, first, second]
    return pl.pallas_call(
        bump_kernel,
        out_shape=(struct((224, 2176), BF16),) * 4,
        grid=(1,),
        in_specs=sides + [first] * 4,
        out_specs=tuple(sides),
        input_output_aliases={0: 0, 1: 1, 2: 2, 3: 3},
        compiler_params=PARAMS,
        cost_estimate=HINT,
    )(x_up, x_down, y_up, y_down, *got)


def spread_kernel(where, a, b, c, *outs):
    value = (a[...].astype(F32) + b[...].astype(F32) + c[...].astype(F32)).astype(BF16)
    for n in range(4):
        piece = jnp.concatenate(
            [value[:, n * 320 : n * 320 + 320], value[:, 1280 + n * 224 : 1280 + n * 224 + 224]], axis=1
        )
        turn = lax.rem(n - where[0] + 4, 4)
        for k in range(4):

            @pl.when(turn == k)
            def _(k=k, piece=piece):
                outs[k][...] = piece


def spread_of(where, parts):
    return pl.pallas_call(
        spread_kernel,
        out_shape=(struct((224, 544), BF16),) * 4,
        grid=(2,),
        in_specs=[SMEM] + [pl.BlockSpec((112, 2176), lambda i: (i, 0))] * 3,
        out_specs=(pl.BlockSpec((112, 544), lambda i: (i, 0)),) * 4,
        compiler_params=PARAMS,
        cost_estimate=LONG,
    )(where, *parts)


def finish_kernel(a0, a1, a2, a3, b0, b1, b2, b3, grad_in, grad_out):
    first = a0[...].astype(F32) + a1[...].astype(F32) + a2[...].astype(F32) + a3[...].astype(F32)
    second = b0[...].astype(F32) + b1[...].astype(F32) + b2[...].astype(F32) + b3[...].astype(F32)
    both = jnp.concatenate([first, second], axis=0)
    grad_in[...] = both[:, 0:320].T.astype(BF16)
    grad_out[...] = both[:, 320:544].astype(BF16)


def finish_of(first, second):
    return pl.pallas_call(
        finish_kernel,
        out_shape=(struct((320, 448), BF16), struct((448, 224), BF16)),
        in_specs=[VMEM] * 8,
        out_specs=(VMEM, VMEM),
        compiler_params=PARAMS,
        cost_estimate=LONG,
    )(*first, *second)


def weight_sum_kernel(parts, out):
    total = parts[0].astype(F32)
    for k in range(1, 4):
        total = total + parts[k].astype(F32)
    out[...] = jnp.zeros_like(out)
    for n in range(16):
        out[n, 0:10, :] = total[n * 10 : n * 10 + 10].astype(BF16)


def weight_sum_of(parts):
    return pl.pallas_call(
        weight_sum_kernel,
        out_shape=struct((16, 16, 1280), BF16),
        in_specs=[VMEM],
        out_specs=VMEM,
        compiler_params=SMALL,
        cost_estimate=HINT,
    )(parts)


def ring_of(parts, shift):
    far = lax.ppermute(parts[2], "seq", shift(2))
    up = lax.ppermute(parts[1], "seq", shift(1))
    down = lax.ppermute(parts[3], "seq", shift(-1))
    return (parts[0], up, down, far)


def order_kernel(target, target_other, context, out, out_other):
    for where, to in ((target, out), (target_other, out_other)):
        pick = jnp.where(iota((1280, 128), 0) == where[...], 1.0, 0.0).astype(BF16)
        to[...] = mm(context[...], pick).T.astype(BF16)


def order_of(target, context):
    target = target.reshape(1, 1280)
    return pl.pallas_call(
        order_kernel,
        out_shape=(struct((640, 192), BF16),) * 2,
        grid=(5,),
        in_specs=[
            pl.BlockSpec((1, 128), lambda i: (0, i)),
            pl.BlockSpec((1, 128), lambda i: (0, i + 5)),
            whole((192, 1280)),
        ],
        out_specs=(pl.BlockSpec((128, 192), lambda i: (i, 0)),) * 2,
        compiler_params=SMALL,
        cost_estimate=LONG,
    )(target, target, context)


def out_weight_kernel(ctx, ctx_other, grad, grad_other, out):
    out[...] = (mm(ctx[...], grad[...]) + mm(ctx_other[...], grad_other[...])).astype(BF16)


def out_weight_of(ctx, ctx_other, grad, grad_other):
    block = pl.BlockSpec((192, 256), lambda i: (0, i))
    return pl.pallas_call(
        out_weight_kernel,
        out_shape=struct((640, 1280), BF16),
        grid=(5,),
        in_specs=[whole((640, 192)), whole((640, 192)), block, block],
        out_specs=pl.BlockSpec((640, 256), lambda i: (0, i)),
        compiler_params=SMALL,
        cost_estimate=HINT,
    )(ctx, ctx_other, grad, grad_other)


def swap(value):
    return lax.ppermute(value, "tp", CORE_SWAP)


def z_blocks(block):
    far = lax.ppermute(block, "tp", z_shift(2))
    behind = lax.ppermute(block, "tp", z_shift(1))
    ahead = lax.ppermute(block, "tp", z_shift(-1))
    return (block, ahead, far, behind)


def z_exchange(parts):
    return lax.all_to_all(parts, "tp", split_axis=0, concat_axis=0, axis_index_groups=Z_GROUPS, tiled=True)


def per_device(
    context,
    residual_in,
    out_weight,
    final_norm_weight,
    final_norm_bias,
    adapter_in,
    adapter_out,
    emb_grad,
    group_offsets,
    group_frames,
    group_owner,
):
    s = lax.axis_index("seq")
    t = lax.axis_index("tp")
    c = t % 2
    ids = jnp.stack([s // 4, s % 4, t // 2, c, s]).astype(jnp.int32)
    context = context.reshape(192, 1280)
    residual_in = residual_in.reshape(192, 1280)

    in_own = adapter_in.T
    in_other = swap(in_own)
    out_other = swap(adapter_out)

    parcels = parcels_of(group_offsets, group_frames, group_owner, emb_grad.T)
    arrived = lax.all_to_all(parcels, "seq", split_axis=0, concat_axis=0, tiled=True)
    context, _ = lax.optimization_barrier((context, parcels))
    stacked_here, normed, inverse = encode_of(context, residual_in, out_weight, final_norm_weight, final_norm_bias)
    rows = z_blocks(stacked_here)
    arrived, in_other, out_other, _ = lax.optimization_barrier((arrived, in_other, out_other, stacked_here))

    keep, give = select_of(ids, group_owner, arrived)
    got = swap(give)
    grad_pair = pair_of(ids, keep, got)
    og = z_exchange(grad_pair)

    place = jnp.arange(1280, dtype=jnp.int32)
    core = (place // 640 + c) % 2
    target = (2 * ((place % 640) // 160) + core) * 10 + ((place % 160) // 10) * 80 + place % 10
    context_keep, context_give = order_of(target, context)
    context_got = swap(context_give)

    rows, _ = lax.optimization_barrier((rows, grad_pair))
    stk, hid_own, hid_other, slope_own, slope_other = preact_of(ids, rows, in_own, in_other)
    stk_other = swap(stk)
    og, _ = lax.optimization_barrier((og, context_got))
    og_other = swap(og)
    row_part, pre_own, send = pre_grad_of(
        og, adapter_out, out_other, in_own, in_other, hid_other, slope_own, slope_other
    )
    recv = swap(send)
    row_parts = z_exchange(row_part.reshape(4, 48, 5120))

    pre_own, _ = lax.optimization_barrier((pre_own, row_part))
    operands = (ids, stk, stk_other, og, og_other, pre_own, hid_own, recv)
    x_far, x_far2, y_far, y_far2 = weight_grads_of(True, *operands)
    got = (
        lax.ppermute(x_far, "seq", x_shift(1)),
        lax.ppermute(x_far2, "seq", x_shift(-1)),
        lax.ppermute(y_far, "seq", y_shift(1)),
        lax.ppermute(y_far2, "seq", y_shift(-1)),
    )
    pre_own, _ = lax.optimization_barrier((pre_own, x_far))
    x_here, x_up, x_down, y_here, y_up, y_down = weight_grads_of(
        False, ids, stk, stk_other, og, og_other, pre_own, hid_own, recv
    )
    x_up, x_down, y_up, y_down = bump_of(x_up, x_down, y_up, y_down, got)
    row_parts, _ = lax.optimization_barrier((row_parts, x_up))

    d_residual = norm_back_of(row_parts, normed, inverse, final_norm_weight)
    residual_other = swap(d_residual)
    weight_part = out_weight_of(context_keep, context_got, d_residual, residual_other)
    residual_late, _ = lax.optimization_barrier((d_residual, weight_part))
    d_context = mm(residual_late, out_weight, 1, 1).astype(BF16)
    y_here, _ = lax.optimization_barrier((y_here, d_context))
    y_next = spread_of(
        ids[1:2], (y_here, lax.ppermute(y_up, "seq", y_shift(1)), lax.ppermute(y_down, "seq", y_shift(-1)))
    )
    x_sums = (x_here, lax.ppermute(x_up, "seq", x_shift(1)), lax.ppermute(x_down, "seq", x_shift(-1)))

    weight_parts, _ = lax.optimization_barrier((z_exchange(weight_part.reshape(4, 160, 1280)), y_next[0]))
    weight_z = weight_sum_of(weight_parts)
    pieces = lax.all_to_all(weight_z, "seq", split_axis=0, concat_axis=0, tiled=True)
    d_out_weight = jnp.sum(pieces.astype(F32), axis=0)[:10]

    x_next = spread_of(ids[0:1], x_sums)
    first = ring_of(x_next, y_shift)
    second = ring_of(y_next, x_shift)
    grad_in, grad_out = finish_of(first, second)

    return (
        d_context.reshape(8, 24, 1280),
        d_residual.reshape(8, 24, 1280),
        d_out_weight,
        grad_in,
        grad_out,
    )


def solution(mesh):
    placed = (
        P("seq", "tp", None),
        P("seq", "tp", None),
        P(),
        P(),
        P(),
        P(None, "tp"),
        P("tp", None),
        P("seq", "tp"),
        P(),
        P(),
        P(),
    )
    return jax.shard_map(
        per_device,
        mesh=mesh,
        in_specs=placed,
        out_specs=(
            P("seq", "tp", None),
            P("seq", "tp", None),
            P(("seq", "tp"), None),
            P("seq", "tp"),
            P("tp", "seq"),
        ),
        check_vma=False,
    )
```
